512 devices in a mesh: dp: 64 (over y, x, core), proto: 8 (over z).
Axes of the slice: x: 4, y: 8, z: 8, core: 2. Of those that a mesh axis runs over, the one named last changes fastest.
Arguments:
- student_features: bfloat16 [8192, 384], P('dp'), may hold values from -160 to 160
- teacher_features: bfloat16 [8192, 384], P('dp'), may hold values from -160 to 160
- prototypes: bfloat16 [65536, 384], P(('dp', 'proto')), may hold values from -160 to 160
Outputs:
- grad_features: float32 [8192, 384], P('dp')
- grad_prototypes: float32 [65536, 384], P(('dp', 'proto'))
- losses: float32 [8192], P('dp')
The draws below stay inside these ranges and needn't reach their ends.
All inputs are finite; a program needn't handle non-finite values.
Results may differ from the reference program's by a relative error of at most 0.0015.
Values may be sent and summed in bfloat16 or wider, within the bound.
A program may use at most 128 MiB of HBM per device.

```python
import math
import jax
import jax.numpy as jnp
from jax import lax

K = 384
P_SIZE = 65536
CROPS = 8192


signal_gain = 4.6


value_bound = 160.0


def shared_signs(key):
    coin_flips = jax.random.randint(key, (K,), 0, 2)
    return (2 * coin_flips - 1).astype(jnp.float32)


def assemble(noise_part, strength, sign_vector, row_top, column_top, row_key, column_key):
    row_count = noise_part.shape[0]
    row_scale = jnp.exp(jax.random.uniform(row_key, (row_count, 1), jnp.float32, 0.0, math.log(row_top)))
    column_scale = jnp.exp(jax.random.uniform(column_key, (1, K), jnp.float32, 0.0, math.log(column_top)))
    values = row_scale * (strength * signal_gain * sign_vector[None, :] + column_scale * noise_part)
    return jnp.clip(values, -value_bound, value_bound).astype(jnp.bfloat16)


def draw_teacher_features(key, part):
    sign_vector = shared_signs(key)
    key = jax.random.fold_in(key, 11)
    subkeys = jax.random.split(key, 4)
    position = jnp.arange(CROPS, dtype=jnp.float32)[:, None] * (1.0 / CROPS)
    noise_part = jnp.clip(jax.random.normal(subkeys[0], (CROPS, K), jnp.float32), -4.5, 4.5)
    strength = jax.random.uniform(subkeys[1], (CROPS, 1), jnp.float32, 0.2, 1.0)
    row_top = 8.0
    column_top = 8.0
    return assemble(noise_part, strength * (1.0 + 2.0 * position), sign_vector, row_top, column_top, subkeys[2], subkeys[3])


def draw_student_features(key, part):
    sign_vector = shared_signs(key)
    key = jax.random.fold_in(key, 13)
    subkeys = jax.random.split(key, 4)
    noise_part = jnp.clip(jax.random.normal(subkeys[0], (CROPS, K), jnp.float32), -4.5, 4.5)
    strength = jax.random.uniform(subkeys[1], (CROPS, 1), jnp.float32, 0.2, 2.0)
    row_top = 8.0
    column_top = 8.0
    return assemble(noise_part, strength, sign_vector, row_top, column_top, subkeys[2], subkeys[3])


def draw_prototypes(key, part):
    sign_vector = shared_signs(key)
    key = jax.random.fold_in(key, 17)
    subkeys = jax.random.split(key, 4)
    noise_part = jnp.clip(jax.random.normal(subkeys[0], (P_SIZE, K), jnp.float32), -4.5, 4.5)
    strength = jax.random.uniform(subkeys[1], (P_SIZE, 1), jnp.float32, -1.5, 1.5)
    row_top = 8.0
    column_top = 8.0
    return assemble(noise_part, strength, sign_vector, row_top, column_top, subkeys[2], subkeys[3])


def setup_inputs(seed: int = 0) -> dict:
    arg_keys = jax.random.split(jax.random.key(seed), 4)
    return {
        "student_features": draw_student_features(jax.random.fold_in(arg_keys[3], 71), 0),
        "teacher_features": draw_teacher_features(jax.random.fold_in(arg_keys[3], 71), 0),
        "prototypes": draw_prototypes(jax.random.fold_in(arg_keys[3], 71), 0),
    }


teacher_temp = 0.07
student_temp = 0.1
norm_eps = 1e-06

def unit_rows(values):
    widened = values.astype(jnp.float32)
    inverse = lax.rsqrt(lax.optimization_barrier(jnp.sum(widened * widened, axis=-1, keepdims=True)) + norm_eps)
    return (widened * inverse, inverse)

def reference(student_features, teacher_features, prototypes):
    block_rows = math.gcd(CROPS, 512)
    blocks = CROPS // block_rows
    proto_unit, proto_inverse = unit_rows(prototypes)
    proto_half = proto_unit.astype(jnp.bfloat16)
    student_unit, student_inverse = unit_rows(student_features)
    student_half = student_unit.astype(jnp.bfloat16)
    teacher_half = unit_rows(teacher_features)[0].astype(jnp.bfloat16)
    teacher_blocks = teacher_half.reshape(blocks, block_rows, K)
    student_blocks = student_half.reshape(blocks, block_rows, K)

    def teacher_exp(crop_block):
        return jnp.exp(jnp.dot(crop_block, proto_half.T, preferred_element_type=jnp.float32) * (1.0 / teacher_temp))

    def first_sum(running, crop_block):
        return (running + lax.optimization_barrier(jnp.sum(teacher_exp(crop_block), axis=0)), None)
    column_total, _ = lax.scan(first_sum, jnp.zeros((P_SIZE,), jnp.float32), teacher_blocks)
    column_scale = 1.0 / column_total
    for iteration in range(2):

        def weighted_sum(running, crop_block, scale_now=column_scale):
            teacher_expo = teacher_exp(crop_block)
            row_scale = 1.0 / lax.optimization_barrier(jnp.sum(teacher_expo * scale_now[None, :], axis=1))
            return (running + lax.optimization_barrier(jnp.sum(teacher_expo * row_scale[:, None], axis=0)), None)
        column_total, _ = lax.scan(weighted_sum, jnp.zeros((P_SIZE,), jnp.float32), teacher_blocks)
        column_scale = 1.0 / column_total

    def final_block(running, paired):
        rows_teacher, rows_student = paired
        scaled = teacher_exp(rows_teacher) * column_scale[None, :]
        target = scaled * (1.0 / lax.optimization_barrier(jnp.sum(scaled, axis=1)))[:, None]
        logits = jnp.dot(rows_student, proto_half.T, preferred_element_type=jnp.float32) * (1.0 / student_temp)
        student_expo = jnp.exp(logits)
        student_total = lax.optimization_barrier(jnp.sum(student_expo, axis=1))
        crop_losses = jnp.log(student_total) - lax.optimization_barrier(jnp.sum(target * logits, axis=1))
        score_grad = ((student_expo / student_total[:, None] - target) * (1.0 / CROPS)).astype(jnp.bfloat16)
        feature_grad = jnp.dot(score_grad, proto_half, preferred_element_type=jnp.float32) * (1.0 / student_temp)
        running = running + jnp.dot(score_grad.T, rows_student, preferred_element_type=jnp.float32)
        return (running, (crop_losses, feature_grad))
    proto_sum, (loss_blocks, grad_blocks) = lax.scan(final_block, jnp.zeros((P_SIZE, K), jnp.float32), (teacher_blocks, student_blocks))
    losses = loss_blocks.reshape(CROPS)
    unit_grad = grad_blocks.reshape(CROPS, K)
    grad_features = student_inverse * (unit_grad - student_unit * lax.optimization_barrier(jnp.sum(student_unit * unit_grad, axis=1, keepdims=True)))
    proto_grad = proto_sum * (1.0 / student_temp)
    grad_prototypes = proto_inverse * (proto_grad - proto_unit * lax.optimization_barrier(jnp.sum(proto_unit * proto_grad, axis=1, keepdims=True)))
    return (grad_features, grad_prototypes, losses)
```

```python
import jax
import jax.numpy as jnp
from jax import lax
from jax.experimental import pallas as pl
from jax.experimental.pallas import tpu as pltpu
from jax.sharding import PartitionSpec as P

NY, NX, NC, NZ = 8, 4, 2, 8
NP = NX * NC
B = 128
K = 384
R = NY * B
C = NP * B
PIECE = B // NZ
CROPS = NY * NX * NC * B
TEACHER = 1.0 / 0.07
STUDENT = 1.0 / 0.1
EPS = 1e-06
MESH = pl.DeviceIdType.MESH
F32, BF16 = jnp.float32, jnp.bfloat16


def unit_rows(values):
    widened = values.astype(F32)
    inverse = lax.rsqrt(jnp.sum(widened * widened, axis=-1, keepdims=True) + EPS)
    return widened * inverse, inverse


def against_rows(a, b):
    return lax.dot_general(a, b, (((1,), (1,)), ((), ())), preferred_element_type=F32)


def project(unit, grad, inverse):
    return inverse * (grad - unit * jnp.sum(unit * grad, axis=1, keepdims=True))


def kernel(
    s_ref, t_ref, p_ref, gf_ref, gp_ref, loss_ref,
    t_all, s_all, s_turned, p_all, e_ref, l_ref, x_ref, g_ref, su_ref, pu_ref, sinv_ref, pinv_ref,
    colx, rowy, rowz, lasty, lastz, col_now, row_now, last_now,
    u_ref, near, zfar, w_ref, yfar, b_ref, zn, gfb, v_ref, vsib, vx,
    ts, tr, ss, sr, ps, pr, xs, xr, ys, yr, zs, zr, us, ur, vs, vr,
):
    dp, z = lax.axis_index("dp"), lax.axis_index("proto")
    core = lax.rem(dp, NC)
    x = lax.rem(lax.div(dp, NC), NX)
    y = lax.div(dp, NC * NX)
    own = core * NX + x

    def at_y(other):
        return ((other * NX + x) * NC + core, z)

    def at_z(other):
        return (dp, other)

    def at_p(other):
        return ((y * NX + lax.rem(other, NX)) * NC + lax.div(other, NX), z)

    def ring(value, size):
        return lax.rem(value + size, size)

    def copy(src, dst, send, recv, device):
        return pltpu.make_async_remote_copy(
            src_ref=src, dst_ref=dst, send_sem=send, recv_sem=recv, device_id=device, device_id_type=MESH
        )

    def each(first, last, body):
        def step(i, carry):
            body(i)
            return carry

        lax.fori_loop(first, last, step, 0)

    barrier = pltpu.get_barrier_semaphore()

    def greet(q):
        for device in (at_y(ring(y + q, NY)), at_p(ring(own + q, NP)), at_z(ring(z + q, NZ))):
            pl.semaphore_signal(barrier, inc=1, device_id=device, device_id_type=MESH)

    each(1, 8, greet)

    t_all[0] = unit_rows(t_ref[...])[0].astype(BF16)
    p_unit, p_inverse = unit_rows(p_ref[...])
    p_all[own] = p_unit.astype(BF16)
    pu_ref[...] = p_unit
    pinv_ref[...] = jnp.broadcast_to(p_inverse, (B, 128))
    s_unit, s_inverse = unit_rows(s_ref[...])
    s_all[0] = s_unit.astype(BF16)
    su_ref[...] = s_unit
    sinv_ref[...] = jnp.broadcast_to(s_inverse, (B, 128))
    pl.semaphore_wait(barrier, 21)

    def rows(who):
        return pl.ds(pl.multiple_of(who * PIECE, PIECE), PIECE)

    def far_copy(ref, send, recv, d):
        part = (d, rows(z))
        return copy(ref.at[0, rows(z)], ref.at[part], send.at[d], recv.at[d], at_y(ring(y - d, NY)))

    def near_copy(ref, send, recv, d):
        return copy(ref.at[0], ref.at[d], send.at[d], recv.at[d], at_y(ring(y - d, NY)))

    def pass_copy(ref, send, recv, j, source, target):
        part = ref.at[pl.ds(3, 3), rows(source)]
        return copy(part, part, send.at[8 + j], recv.at[8 + j], at_z(target))

    def near_d(i):
        return ring((lax.div(i, 2) + 1) * (1 - 2 * lax.rem(i, 2)), NY)

    def gather_start(ref, send, recv):
        each(3, 6, lambda d: far_copy(ref, send, recv, d).start())
        each(0, 4, lambda i: near_copy(ref, send, recv, near_d(i)).start())

    def gather_pass(ref, send, recv):
        each(3, 6, lambda d: far_copy(ref, send, recv, d).wait_recv())
        each(1, 8, lambda j: pass_copy(ref, send, recv, j, z, ring(z + j, NZ)).start())

    def gather_far(ref, send, recv):
        each(1, 8, lambda j: pass_copy(ref, send, recv, j, ring(z - j, NZ), ring(z + j, NZ)).wait_recv())

    def gather_sent(ref, send, recv):
        each(3, 6, lambda d: far_copy(ref, send, recv, d).wait_send())
        each(0, 4, lambda i: near_copy(ref, send, recv, near_d(i)).wait_send())
        each(1, 8, lambda j: pass_copy(ref, send, recv, j, z, ring(z + j, NZ)).wait_send())

    def x_copy(j, source, target):
        part = p_all.at[core * NX + source]
        return copy(part, part, ps.at[j], pr.at[j], at_p(core * NX + target))

    def sib_copy(j, who):
        part = p_all.at[who * NX + ring(x - j, NX)]
        return copy(part, part, ps.at[4 + j], pr.at[4 + j], at_p((1 - core) * NX + x))

    each(1, 4, lambda j: x_copy(j, x, ring(x + j, NX)).start())
    gather_start(t_all, ts, tr)
    sib_copy(0, core).start()
    gather_pass(t_all, ts, tr)

    def hand_over(j):
        x_copy(j, ring(x - j, NX), ring(x + j, NX)).wait_recv()
        sib_copy(j, core).start()

    each(1, 4, hand_over)
    each(0, 4, lambda j: sib_copy(j, 1 - core).wait_recv())

    def crop_rows(d):
        return pl.ds(pl.multiple_of(d * B, B), B)

    def proto_pair(n):
        return p_all[2 * n : 2 * n + 2].reshape(2 * B, K)

    col_now[...] = jnp.zeros((8, C), F32)

    def teacher_block(d):
        block = t_all[d]
        for n in range(C // 256):
            lanes = slice(n * 256, (n + 1) * 256)
            expo = jnp.exp(against_rows(block, proto_pair(n)) * TEACHER)
            e_ref[crop_rows(d), lanes] = expo
            col_now[:, lanes] += jnp.sum(expo.reshape(B // 8, 8, 256), axis=0)

    teacher_block(0)

    def near_teacher(i):
        d = near_d(i)
        near_copy(t_all, ts, tr, d).wait_recv()
        teacher_block(d)

    each(0, 4, near_teacher)
    gather_start(s_all, ss, sr)
    gather_far(t_all, ts, tr)
    each(3, 6, teacher_block)

    def swap_start(buf, send, recv, mine, at):
        part = buf.at[mine]
        each(1, 8, lambda q: copy(part, part, send.at[q], recv.at[mine], at(ring(mine + q, 8))).start())

    def swap_wait(buf, send, recv, mine, at):
        def one(q):
            source = ring(mine + q, 8)
            part = buf.at[source]
            copy(part, part, send.at[q], recv.at[source], at(source)).wait_recv()

        each(1, 8, one)
        total = buf[0]
        for i in range(1, 8):
            total = total + buf[i]
        return total

    def swap_sent(buf, send, recv, mine, at):
        part = buf.at[mine]
        each(1, 8, lambda q: copy(part, part, send.at[q], recv.at[mine], at(ring(mine + q, 8))).wait_send())

    def col_swap(it):
        return colx.at[it], xs.at[it], xr.at[it], own, at_p

    def y_swap(it):
        return (rowy.at[it] if it < 2 else lasty), ys.at[it], yr.at[it], y, at_y

    def z_swap(it):
        return (rowz.at[it] if it < 2 else lastz), zs.at[it], zr.at[it], z, at_z

    def lane_rows(tile):
        return jnp.sum(tile.T, axis=0, keepdims=True)

    def down(vector):
        return jnp.broadcast_to(vector, (B, B)).T

    def lane_tile(k):
        return slice(k * B, (k + 1) * B)

    def student_block(d):
        block = s_all[d]
        total = jnp.zeros((B, B), F32)
        for n in range(C // 256):
            lanes = slice(n * 256, (n + 1) * 256)
            logits = against_rows(block, proto_pair(n)) * STUDENT
            expo = jnp.exp(logits)
            l_ref[crop_rows(d), lanes] = logits
            x_ref[crop_rows(d), lanes] = expo
            total = total + expo[:, :B] + expo[:, B:]
        lasty[y, pl.ds(16 + ring(y + d, NY), 1), :] = lane_rows(total)
        s_turned[:, crop_rows(d)] = block.T

    def near_student(i):
        d = near_d(i)
        near_copy(s_all, ss, sr, d).wait_recv()
        student_block(d)

    def weigh_rows(it):
        scale = col_now[:, :B]

        def block(d):
            total = jnp.zeros((B, B), F32)
            for k in range(NP):
                total = total + e_ref[crop_rows(d), lane_tile(k)] * scale[k : k + 1, :]
            rowy[it, y, pl.ds(ring(y + d, NY), 1), :] = lane_rows(total)

        each(0, NY, block)

    def weigh_columns(it):
        def block(d, totals):
            scale = down(row_now[pl.ds(ring(y + d, NY), 1), :])
            return tuple(
                totals[k]
                + jnp.sum((e_ref[crop_rows(d), lane_tile(k)] * scale).reshape(B // 8, 8, B), axis=0)
                for k in range(NP)
            )

        totals = lax.fori_loop(0, NY, block, (jnp.zeros((8, B), F32),) * NP)
        for k in range(NP):
            colx[it, own, k : k + 1, :] = jnp.sum(totals[k], axis=0, keepdims=True)

    for k in range(NP):
        colx[0, own, k : k + 1, :] = jnp.sum(col_now[:, lane_tile(k)], axis=0, keepdims=True)
    swap_start(*col_swap(0))
    gather_pass(s_all, ss, sr)
    student_block(0)
    col_now[:, :B] = 1.0 / swap_wait(*col_swap(0))
    for it in range(2):
        weigh_rows(it)
        swap_start(*y_swap(it))
        if it == 0:
            near_student(0)
        else:
            student_block(3)
        rowz[it, z] = swap_wait(*y_swap(it))
        swap_start(*z_swap(it))
        if it == 0:
            near_student(1)
            near_student(2)
        else:
            student_block(4)
        row_now[...] = 1.0 / swap_wait(*z_swap(it))
        weigh_columns(it + 1)
        swap_start(*col_swap(it + 1))
        if it == 0:
            near_student(3)
            gather_far(s_all, ss, sr)
        else:
            student_block(5)
        col_now[:, :B] = 1.0 / swap_wait(*col_swap(it + 1))

    def last_rows(d):
        scale = col_now[:, :B]
        total, mixed = jnp.zeros((B, B), F32), jnp.zeros((B, B), F32)
        for k in range(NP):
            scaled = e_ref[crop_rows(d), lane_tile(k)] * scale[k : k + 1, :]
            total = total + scaled
            mixed = mixed + scaled * l_ref[crop_rows(d), lane_tile(k)]
        lasty[y, pl.ds(ring(y + d, NY), 1), :] = lane_rows(total)
        lasty[y, pl.ds(8 + ring(y + d, NY), 1), :] = lane_rows(mixed)

    each(0, NY, last_rows)
    swap_start(*y_swap(2))
    lastz[z] = swap_wait(*y_swap(2))
    swap_start(*z_swap(2))
    last_now[...] = swap_wait(*z_swap(2))
    mine = pl.ds(y, 1)
    row_total, mixed_total, student_total = last_now[0:8], last_now[8:16], last_now[16:24]
    row_now[...] = jnp.log(student_total) - mixed_total / row_total
    loss_ref[...] = row_now[mine, :]
    last_now[0:8] = 1.0 / row_total
    last_now[16:24] = 1.0 / student_total

    def grad_block(d):
        b = ring(y + d, NY)
        scale = col_now[:, :B]
        row_scale, student_scale = down(last_now[pl.ds(b, 1), :]), down(last_now[pl.ds(16 + b, 1), :])
        for k in range(NP):
            target = e_ref[crop_rows(d), lane_tile(k)] * scale[k : k + 1, :] * row_scale
            g_ref[crop_rows(d), lane_tile(k)] = (
                x_ref[crop_rows(d), lane_tile(k)] * student_scale - target
            ).astype(BF16)
        u_ref[d] = jnp.dot(g_ref[crop_rows(d), :], p_all[...].reshape(C, K), preferred_element_type=F32)

    def u_far(j, source, target):
        return copy(
            u_ref.at[pl.ds(3, 3), rows(target)], zfar.at[source], us.at[j], ur.at[j], at_z(target)
        )

    def u_near(d):
        return copy(u_ref.at[d], near.at[d], us.at[8 + d], ur.at[8 + d], at_y(ring(y + d, NY)))

    def u_sum(k):
        return copy(w_ref.at[k], yfar.at[k], us.at[16 + k], ur.at[16 + k], at_y(ring(y + 3 + k, NY)))

    def u_piece(j, source, target):
        return copy(b_ref.at[rows(target)], zn.at[source], us.at[24 + j], ur.at[24 + j], at_z(target))

    def u_all(j, source, target):
        part = gfb.at[rows(source)]
        return copy(part, part, us.at[32 + j], ur.at[32 + j], at_z(target))

    def z_start(make):
        each(1, NZ, lambda j: make(j, z, ring(z + j, NZ)).start())

    def z_wait(make):
        each(1, NZ, lambda j: make(j, ring(z - j, NZ), ring(z + j, NZ)).wait_recv())

    def z_sent(make):
        each(1, NZ, lambda j: make(j, z, ring(z + j, NZ)).wait_send())

    each(3, 6, grad_block)
    z_start(u_far)

    def near_grad(i):
        d = near_d(i)
        grad_block(d)
        u_near(d).start()

    each(0, 4, near_grad)
    grad_block(0)

    def proto_grad(half):
        def pair(n):
            first = pl.multiple_of((half * 2 + n) * 256, 256)
            both = jnp.dot(s_turned[...], g_ref[:, pl.ds(first, 256)], preferred_element_type=F32)
            v_ref[half * NX + 2 * n] = both[:, :B]
            v_ref[half * NX + 2 * n + 1] = both[:, B:]

        each(0, 2, pair)

    def v_sib(who):
        return copy(v_ref.at[pl.ds(who * NX, NX)], vsib, vs.at[0], vr.at[0], at_p((1 - core) * NX + x))

    def v_x(j, source, target):
        return copy(
            v_ref.at[core * NX + target], vx.at[source], vs.at[j], vr.at[j], at_p(core * NX + target)
        )

    proto_grad(1 - core)
    v_sib(1 - core).start()
    proto_grad(core)

    z_wait(u_far)
    zfar[z] = u_ref[pl.ds(3, 3), rows(z)]
    total = zfar[0]
    for i in range(1, NZ):
        total = total + zfar[i]
    w_ref[...] = total
    each(0, 3, lambda k: u_sum(k).start())

    v_sib(1 - core).wait_recv()

    def add_sibling(i):
        v_ref[core * NX + i] += vsib[i]

    each(0, NX, add_sibling)
    each(1, NX, lambda j: v_x(j, x, ring(x + j, NX)).start())

    each(0, 4, lambda i: u_near(near_d(i)).wait_recv())
    b_ref[...] = u_ref[0] + near[1] + near[2] + near[6] + near[7]
    z_start(u_piece)

    each(1, NX, lambda j: v_x(j, ring(x - j, NX), ring(x + j, NX)).wait_recv())
    vx[x] = v_ref[own]
    proto_sum = (vx[0] + vx[1] + vx[2] + vx[3]).T * (STUDENT / CROPS)
    gp_ref[...] = project(pu_ref[...], proto_sum, pinv_ref[:, 0:1])

    z_wait(u_piece)
    each(0, 3, lambda k: u_sum(k).wait_recv())
    zn[z] = b_ref[rows(z)]
    total = yfar[0] + yfar[1] + yfar[2]
    for i in range(NZ):
        total = total + zn[i]
    gfb[rows(z)] = project(su_ref[rows(z)], total * (STUDENT / CROPS), sinv_ref[rows(z), 0:1])
    z_start(u_all)
    z_wait(u_all)
    gf_ref[...] = gfb[...]

    each(1, 4, lambda j: x_copy(j, x, ring(x + j, NX)).wait_send())
    each(0, 4, lambda j: sib_copy(j, core).wait_send())
    gather_sent(t_all, ts, tr)
    gather_sent(s_all, ss, sr)
    for it in range(3):
        swap_sent(*col_swap(it))
        swap_sent(*y_swap(it))
        swap_sent(*z_swap(it))
    z_sent(u_far)
    each(0, 4, lambda i: u_near(near_d(i)).wait_send())
    each(0, 3, lambda k: u_sum(k).wait_send())
    z_sent(u_piece)
    z_sent(u_all)
    v_sib(1 - core).wait_send()
    each(1, NX, lambda j: v_x(j, x, ring(x + j, NX)).wait_send())


def shards(student_features, teacher_features, prototypes):
    vmem = pl.BlockSpec(memory_space=pltpu.VMEM)
    dma = pltpu.SemaphoreType.DMA
    grad_features, grad_prototypes, losses = pl.pallas_call(
        kernel,
        out_shape=(
            jax.ShapeDtypeStruct((B, K), F32),
            jax.ShapeDtypeStruct((B, K), F32),
            jax.ShapeDtypeStruct((1, B), F32),
        ),
        in_specs=[vmem] * 3,
        out_specs=(vmem,) * 3,
        scratch_shapes=[
            pltpu.VMEM((NY, B, K), BF16),
            pltpu.VMEM((NY, B, K), BF16),
            pltpu.VMEM((K, R), BF16),
            pltpu.VMEM((NP, B, K), BF16),
            pltpu.VMEM((R, C), F32),
            pltpu.VMEM((R, C), F32),
            pltpu.VMEM((R, C), F32),
            pltpu.VMEM((R, C), BF16),
            pltpu.VMEM((B, K), F32),
            pltpu.VMEM((B, K), F32),
            pltpu.VMEM((B, 128), F32),
            pltpu.VMEM((B, 128), F32),
            pltpu.VMEM((3, 8, 8, 128), F32),
            pltpu.VMEM((2, 8, 8, 128), F32),
            pltpu.VMEM((2, 8, 8, 128), F32),
            pltpu.VMEM((8, 24, 128), F32),
            pltpu.VMEM((8, 24, 128), F32),
            pltpu.VMEM((8, C), F32),
            pltpu.VMEM((8, 128), F32),
            pltpu.VMEM((24, 128), F32),
            pltpu.VMEM((NY, B, K), F32),
            pltpu.VMEM((NY, B, K), F32),
            pltpu.VMEM((NZ, 3, PIECE, K), F32),
            pltpu.VMEM((3, PIECE, K), F32),
            pltpu.VMEM((3, PIECE, K), F32),
            pltpu.VMEM((B, K), F32),
            pltpu.VMEM((NZ, PIECE, K), F32),
            pltpu.VMEM((B, K), F32),
            pltpu.VMEM((NP, K, B), F32),
            pltpu.VMEM((NX, K, B), F32),
            pltpu.VMEM((NX, K, B), F32),
            dma((16,)), dma((16,)),
            dma((16,)), dma((16,)),
            dma((8,)), dma((8,)),
            dma((3, 8)), dma((3, 8)),
            dma((3, 8)), dma((3, 8)),
            dma((3, 8)), dma((3, 8)),
            dma((40,)), dma((40,)),
            dma((4,)), dma((4,)),
        ],
        compiler_params=pltpu.CompilerParams(
            collective_id=0, has_side_effects=True, vmem_limit_bytes=50 * 1024 * 1024
        ),
        name="dino_head",
    )(student_features, teacher_features, prototypes)
    return grad_features, grad_prototypes, losses.reshape(B)


def solution(mesh):
    in_specs = (P("dp", None), P("dp", None), P(("dp", "proto"), None))
    out_specs = (P("dp", None), P(("dp", "proto"), None), P("dp"))
    return jax.shard_map(shards, mesh=mesh, in_specs=in_specs, out_specs=out_specs, check_vma=False)
```

```python
import jax
import jax.numpy as jnp
from jax import lax
from jax.experimental import pallas as pl
from jax.experimental.pallas import tpu as pltpu
from jax.sharding import PartitionSpec as P

NY, NX, NC, NZ = 8, 4, 2, 8
NP = NX * NC
B = 128
K = 384
R = NY * B
C = NP * B
PIECE = B // NZ
CROPS = NY * NX * NC * B
TEACHER = 1.0 / 0.07
STUDENT = 1.0 / 0.1
EPS = 1e-06
MESH = pl.DeviceIdType.MESH
F32, BF16 = jnp.float32, jnp.bfloat16


def unit_rows(values):
    widened = values.astype(F32)
    inverse = lax.rsqrt(jnp.sum(widened * widened, axis=-1, keepdims=True) + EPS)
    return widened * inverse, inverse


def against_rows(a, b):
    return lax.dot_general(a, b, (((1,), (1,)), ((), ())), preferred_element_type=F32)


def project(unit, grad, inverse):
    return inverse * (grad - unit * jnp.sum(unit * grad, axis=1, keepdims=True))


def kernel(
    s_hbm, t_hbm, p_hbm, gf_ref, gp_ref, loss_ref,
    s_ref, t_ref, p_ref,
    t_all, s_all, s_turned, p_all, e_ref, l_ref, x_ref, g_ref, su_ref, pu_ref, sinv_ref, pinv_ref,
    colx, rowy, rowz, lasty, lastz, col_now, row_now, last_now,
    lo_ref, down_ref, us_ref, s_near_in, s_zfar, s_w, s_yfar, s_b, s_zn,
    ut_ref, t_near_in, t_zfar, t_w, t_yfar, t_b, t_zn, gfb, v_ref, vsib, vx,
    ins, ts, tr, ss, sr, ps, pr, xs, xr, ys, yr, zs, zr, uss, usr, uts, utr, gs, gr, vs, vr,
):
    dp, z = lax.axis_index("dp"), lax.axis_index("proto")
    core = lax.rem(dp, NC)
    x = lax.rem(lax.div(dp, NC), NX)
    y = lax.div(dp, NC * NX)
    own = core * NX + x

    def at_y(other):
        return ((other * NX + x) * NC + core, z)

    def at_z(other):
        return (dp, other)

    def at_p(other):
        return ((y * NX + lax.rem(other, NX)) * NC + lax.div(other, NX), z)

    def ring(value, size):
        return lax.rem(value + size, size)

    def copy(src, dst, send, recv, device):
        return pltpu.make_async_remote_copy(
            src_ref=src, dst_ref=dst, send_sem=send, recv_sem=recv, device_id=device, device_id_type=MESH
        )

    def each(first, last, body):
        def step(i, carry):
            body(i)
            return carry

        lax.fori_loop(first, last, step, 0)

    loads = [
        pltpu.make_async_copy(far, here, ins.at[i])
        for i, (far, here) in enumerate(((t_hbm, t_ref), (p_hbm, p_ref), (s_hbm, s_ref)))
    ]
    for load in loads:
        load.start()

    barrier = pltpu.get_barrier_semaphore()

    def greet(q):
        for device in (at_y(ring(y + q, NY)), at_p(ring(own + q, NP)), at_z(ring(z + q, NZ))):
            pl.semaphore_signal(barrier, inc=1, device_id=device, device_id_type=MESH)

    each(1, 8, greet)

    for load in loads:
        load.wait()
    t_all[0] = unit_rows(t_ref[...])[0].astype(BF16)
    p_unit, p_inverse = unit_rows(p_ref[...])
    p_all[own] = p_unit.astype(BF16)
    pu_ref[...] = p_unit
    pinv_ref[...] = jnp.broadcast_to(p_inverse, (B, 128))
    s_unit, s_inverse = unit_rows(s_ref[...])
    s_all[0] = s_unit.astype(BF16)
    su_ref[...] = s_unit
    sinv_ref[...] = jnp.broadcast_to(s_inverse, (B, 128))
    pl.semaphore_wait(barrier, 21)

    log = []

    class Copies:
        def __init__(self, first, last, out, into):
            self.first, self.last, self.out, self.into = first, last, out, into
            self.left = set(range(first, last))

        def start(self):
            log.append(self)
            each(self.first, self.last, lambda i: self.out(i).start())

        def start_one(self, i):
            if self not in log:
                log.append(self)
            self.out(i).start()

        def recv(self):
            self.left.clear()
            each(self.first, self.last, lambda i: self.into(i).wait_recv())

        def recv_one(self, i):
            if isinstance(i, int):
                self.left.discard(i)
            else:
                self.left.clear()
            self.into(i).wait_recv()

        def sent(self):
            each(self.first, self.last, lambda i: self.out(i).wait_send())

    def rows(who):
        return pl.ds(pl.multiple_of(who * PIECE, PIECE), PIECE)

    def crop_rows(d):
        return pl.ds(pl.multiple_of(d * B, B), B)

    def near_d(i):
        return ring((lax.div(i, 2) + 1) * (1 - 2 * lax.rem(i, 2)), NY)

    def over_z(make):
        return Copies(1, NZ, lambda j: make(j, z, ring(z + j, NZ)), lambda j: make(j, ring(z - j, NZ), ring(z + j, NZ)))

    def gather(ref, send, recv):
        def far_copy(d):
            return copy(
                ref.at[0, rows(z)], ref.at[d, rows(z)], send.at[d], recv.at[d], at_y(ring(y - d, NY))
            )

        def near_copy(i):
            d = near_d(i)
            return copy(ref.at[0], ref.at[d], send.at[d], recv.at[d], at_y(ring(y - d, NY)))

        def pass_copy(j, source, target):
            part = ref.at[pl.ds(3, 3), rows(source)]
            return copy(part, part, send.at[8 + j], recv.at[8 + j], at_z(target))

        return Copies(3, 6, far_copy, far_copy), Copies(0, 4, near_copy, near_copy), over_z(pass_copy)

    t_far, t_near, t_pass = gather(t_all, ts, tr)
    s_far, s_near, s_pass = gather(s_all, ss, sr)

    def x_copy(j, source, target):
        part = p_all.at[core * NX + source]
        return copy(part, part, ps.at[j], pr.at[j], at_p(core * NX + target))

    def over_x(make):
        return Copies(1, NX, lambda j: make(j, x, ring(x + j, NX)), lambda j: make(j, ring(x - j, NX), ring(x + j, NX)))

    def sib_copy(j, who):
        part = p_all.at[who * NX + ring(x - j, NX)]
        return copy(part, part, ps.at[4 + j], pr.at[4 + j], at_p((1 - core) * NX + x))

    p_x = over_x(x_copy)
    p_own = Copies(0, 1, lambda j: sib_copy(j, core), lambda j: sib_copy(j, 1 - core))
    p_passed = Copies(1, NX, lambda j: sib_copy(j, core), lambda j: sib_copy(j, 1 - core))

    p_x.start()
    t_far.start()
    t_near.start()
    p_own.start()
    s_far.start()
    t_far.recv()
    t_pass.start()
    p_x.recv()
    p_passed.start()
    s_far.recv()
    p_own.recv()
    p_passed.recv()
    s_pass.start()
    s_near.start()

    def proto_pair(n):
        return p_all[2 * n : 2 * n + 2].reshape(2 * B, K)

    col_now[...] = jnp.zeros((8, C), F32)

    def teacher_block(d):
        block = t_all[d]
        for n in range(C // 256):
            lanes = slice(n * 256, (n + 1) * 256)
            expo = jnp.exp(against_rows(block, proto_pair(n)) * TEACHER)
            e_ref[crop_rows(d), lanes] = expo
            col_now[:, lanes] += jnp.sum(expo.reshape(B // 8, 8, 256), axis=0)

    teacher_block(0)

    def near_teacher(i):
        t_near.recv_one(i)
        teacher_block(near_d(i))

    each(0, 4, near_teacher)
    t_pass.recv()
    each(3, 6, teacher_block)

    class Swap(Copies):
        def __init__(self, buf, send, recv, mine, at):
            def out(q):
                return copy(buf.at[mine], buf.at[mine], send.at[q], recv.at[mine], at(ring(mine + q, 8)))

            def into(q):
                source = ring(mine + q, 8)
                return copy(buf.at[source], buf.at[source], send.at[q], recv.at[source], at(source))

            super().__init__(1, 8, out, into)
            self.buf = buf

        def start(self):
            log.append(self)
            for q in (4, 3, 5, 2, 6, 1, 7):
                self.out(q).start()

        def total(self):
            self.left.clear()
            for q in (1, 7, 2, 6, 3, 5, 4):
                self.into(q).wait_recv()
            total = self.buf[0]
            for i in range(1, 8):
                total = total + self.buf[i]
            return total

    col_swap = [Swap(colx.at[it], xs.at[it], xr.at[it], own, at_p) for it in range(3)]
    y_swap = [Swap(rowy.at[it], ys.at[it], yr.at[it], y, at_y) for it in range(2)]
    z_swap = [Swap(rowz.at[it], zs.at[it], zr.at[it], z, at_z) for it in range(2)]
    last_y = Swap(lasty, ys.at[2], yr.at[2], y, at_y)
    last_z = Swap(lastz, zs.at[2], zr.at[2], z, at_z)

    def lane_rows(tile):
        return jnp.sum(tile.T, axis=0, keepdims=True)

    def down(vector):
        return jnp.broadcast_to(vector, (B, B)).T

    def lane_tile(k):
        return slice(k * B, (k + 1) * B)

    def split(d, lanes, values):
        high = values.astype(BF16)
        g_ref[crop_rows(d), lanes] = high
        lo_ref[:, lanes] = (values - high.astype(F32)).astype(BF16)

    def split_times_protos(d):
        protos = p_all[...].reshape(C, K)
        return jnp.dot(g_ref[crop_rows(d), :], protos, preferred_element_type=F32) + jnp.dot(
            lo_ref[...], protos, preferred_element_type=F32
        )

    class Reduce:
        def __init__(self, u, near, zfar, w, yfar, b, zn, send, recv):
            self.bufs = u, near, zfar, w, yfar, b, zn

            def far_copy(j, source, target):
                part = u.at[pl.ds(3, 3), rows(target)]
                return copy(part, zfar.at[source], send.at[j], recv.at[j], at_z(target))

            def near_copy(i):
                d = near_d(i)
                return copy(u.at[d], near.at[i], send.at[8 + i], recv.at[8 + i], at_y(ring(y + d, NY)))

            def sum_copy(k):
                to = at_y(ring(y + 3 + k, NY))
                return copy(w.at[k], yfar.at[k], send.at[12 + k], recv.at[12 + k], to)

            def piece_copy(j, source, target):
                return copy(b.at[rows(target)], zn.at[source], send.at[16 + j], recv.at[16 + j], at_z(target))

            self.far, self.piece = over_z(far_copy), over_z(piece_copy)
            self.near, self.sum = Copies(0, 4, near_copy, near_copy), Copies(0, 3, sum_copy, sum_copy)

        def far_sums(self):
            u, _, zfar, w, _, _, _ = self.bufs
            self.far.recv()
            zfar[z] = u[pl.ds(3, 3), rows(z)]
            total = zfar[0]
            for i in range(1, NZ):
                total = total + zfar[i]
            w[...] = total
            self.sum.start()

        def near_sums(self):
            u, near, _, _, _, b, _ = self.bufs
            self.near.recv()
            b[...] = u[0] + near[0] + near[1] + near[2] + near[3]
            self.piece.start()

        def result(self):
            _, _, _, _, yfar, b, zn = self.bufs
            self.piece.recv()
            self.sum.recv()
            zn[z] = b[rows(z)]
            total = yfar[0] + yfar[1] + yfar[2]
            for i in range(NZ):
                total = total + zn[i]
            return total

    s_reduce = Reduce(us_ref, s_near_in, s_zfar, s_w, s_yfar, s_b, s_zn, uss, usr)
    t_reduce = Reduce(ut_ref, t_near_in, t_zfar, t_w, t_yfar, t_b, t_zn, uts, utr)
    us_near = s_reduce.near

    def student_block(d):
        block = s_all[d]
        total = jnp.zeros((B, B), F32)
        for n in range(C // 256):
            lanes = slice(n * 256, (n + 1) * 256)
            logits = against_rows(block, proto_pair(n)) * STUDENT
            expo = jnp.exp(logits)
            l_ref[crop_rows(d), lanes] = logits
            x_ref[crop_rows(d), lanes] = expo
            split(d, lanes, expo)
            total = total + expo[:, :B] + expo[:, B:]
        lasty[y, pl.ds(16 + ring(y + d, NY), 1), :] = lane_rows(total)
        s_turned[:, crop_rows(d)] = block.T
        us_ref[d] = split_times_protos(d)

    def near_student(i):
        s_near.recv_one(i)
        student_block(near_d(i))
        us_near.start_one(i)

    def weigh_rows(it):
        scale = col_now[:, :B]

        def block(d):
            total = jnp.zeros((B, B), F32)
            for k in range(NP):
                total = total + e_ref[crop_rows(d), lane_tile(k)] * scale[k : k + 1, :]
            rowy[it, y, pl.ds(ring(y + d, NY), 1), :] = lane_rows(total)

        each(0, NY, block)

    def weigh_columns(it):
        def block(d, totals):
            scale = down(row_now[pl.ds(ring(y + d, NY), 1), :])
            return tuple(
                totals[k]
                + jnp.sum((e_ref[crop_rows(d), lane_tile(k)] * scale).reshape(B // 8, 8, B), axis=0)
                for k in range(NP)
            )

        totals = lax.fori_loop(0, NY, block, (jnp.zeros((8, B), F32),) * NP)
        for k in range(NP):
            colx[it, own, k : k + 1, :] = jnp.sum(totals[k], axis=0, keepdims=True)

    for k in range(NP):
        colx[0, own, k : k + 1, :] = jnp.sum(col_now[:, lane_tile(k)], axis=0, keepdims=True)
    col_swap[0].start()
    student_block(0)
    col_now[:, :B] = 1.0 / col_swap[0].total()
    for it in range(2):
        weigh_rows(it)
        y_swap[it].start()
        if it == 0:
            near_student(0)
            near_student(1)
        else:
            student_block(5)
            s_reduce.far.start()
        rowz[it, z] = y_swap[it].total()
        z_swap[it].start()
        if it == 0:
            near_student(2)
            near_student(3)
        row_now[...] = 1.0 / z_swap[it].total()
        weigh_columns(it + 1)
        col_swap[it + 1].start()
        if it == 0:
            s_pass.recv()
            student_block(3)
            student_block(4)
        col_now[:, :B] = 1.0 / col_swap[it + 1].total()

    def last_rows(d):
        scale = col_now[:, :B]
        total, mixed = jnp.zeros((B, B), F32), jnp.zeros((B, B), F32)
        for k in range(NP):
            scaled = e_ref[crop_rows(d), lane_tile(k)] * scale[k : k + 1, :]
            total = total + scaled
            mixed = mixed + scaled * l_ref[crop_rows(d), lane_tile(k)]
        lasty[y, pl.ds(ring(y + d, NY), 1), :] = lane_rows(total)
        lasty[y, pl.ds(8 + ring(y + d, NY), 1), :] = lane_rows(mixed)

    each(0, NY, last_rows)
    last_y.start()

    def teacher_grad(d):
        scale = col_now[:, :B]
        for k in range(NP):
            split(d, lane_tile(k), e_ref[crop_rows(d), lane_tile(k)] * scale[k : k + 1, :])
        ut_ref[d] = split_times_protos(d)

    each(3, 6, teacher_grad)
    t_reduce.far.start()

    def near_grad(i):
        teacher_grad(near_d(i))
        t_reduce.near.out(i).start()

    log.append(t_reduce.near)
    each(0, 4, near_grad)
    lastz[z] = last_y.total()
    last_z.start()
    teacher_grad(0)
    s_reduce.near_sums()
    s_reduce.far_sums()
    last_now[...] = last_z.total()
    row_total, mixed_total, student_total = last_now[0:8], last_now[8:16], last_now[16:24]
    row_now[...] = jnp.log(student_total) - mixed_total / row_total
    loss_ref[...] = row_now[pl.ds(y, 1), :]
    last_now[0:8] = 1.0 / row_total
    last_now[16:24] = 1.0 / student_total
    down_ref[0] = down(last_now[pl.ds(y, 1), :])
    down_ref[1] = down(last_now[pl.ds(16 + y, 1), :])

    def grad_block(d):
        b = ring(y + d, NY)
        scale = col_now[:, :B]
        row_scale, student_scale = down(last_now[pl.ds(b, 1), :]), down(last_now[pl.ds(16 + b, 1), :])
        for k in range(NP):
            target = e_ref[crop_rows(d), lane_tile(k)] * scale[k : k + 1, :] * row_scale
            g_ref[crop_rows(d), lane_tile(k)] = (
                x_ref[crop_rows(d), lane_tile(k)] * student_scale - target
            ).astype(BF16)

    each(0, NY, grad_block)

    def proto_grad(half):
        def pair(n):
            first = pl.multiple_of((half * 2 + n) * 256, 256)
            both = jnp.dot(s_turned[...], g_ref[:, pl.ds(first, 256)], preferred_element_type=F32)
            v_ref[half * NX + 2 * n] = both[:, :B]
            v_ref[half * NX + 2 * n + 1] = both[:, B:]

        each(0, 2, pair)

    def v_sib_copy(who):
        return copy(v_ref.at[pl.ds(who * NX, NX)], vsib, vs.at[0], vr.at[0], at_p((1 - core) * NX + x))

    def v_x_copy(j, source, target):
        return copy(
            v_ref.at[core * NX + target], vx.at[source], vs.at[j], vr.at[j], at_p(core * NX + target)
        )

    v_sib = Copies(0, 1, lambda i: v_sib_copy(1 - core), lambda i: v_sib_copy(1 - core))
    v_x = over_x(v_x_copy)

    proto_grad(1 - core)
    v_sib.start()
    proto_grad(core)

    v_sib.recv()

    def add_sibling(i):
        v_ref[core * NX + i] += vsib[i]

    each(0, NX, add_sibling)
    v_x.start()
    t_reduce.near_sums()
    t_reduce.far_sums()

    v_x.recv()
    vx[x] = v_ref[own]
    proto_sum = (vx[0] + vx[1] + vx[2] + vx[3]).T * (STUDENT / CROPS)
    gp_ref[...] = project(pu_ref[...], proto_sum, pinv_ref[:, 0:1])
    student_part = s_reduce.result() * down_ref[1, rows(z), 0:1]
    teacher_part = t_reduce.result() * down_ref[0, rows(z), 0:1]
    unit_grad = (student_part - teacher_part) * (STUDENT / CROPS)
    gfb[rows(z)] = project(su_ref[rows(z)], unit_grad, sinv_ref[rows(z), 0:1])

    def all_copy(j, source, target):
        part = gfb.at[rows(source)]
        return copy(part, part, gs.at[j], gr.at[j], at_z(target))

    every = over_z(all_copy)
    every.start()
    every.recv()
    gf_ref[...] = gfb[...]

    for group in log:
        group.sent()


def reduce_shapes():
    return [
        pltpu.VMEM((NY, B, K), F32),
        pltpu.VMEM((4, B, K), F32),
        pltpu.VMEM((NZ, 3, PIECE, K), F32),
        pltpu.VMEM((3, PIECE, K), F32),
        pltpu.VMEM((3, PIECE, K), F32),
        pltpu.VMEM((B, K), F32),
        pltpu.VMEM((NZ, PIECE, K), F32),
    ]


def shards(student_features, teacher_features, prototypes):
    vmem = pl.BlockSpec(memory_space=pltpu.VMEM)
    dma = pltpu.SemaphoreType.DMA
    grad_features, grad_prototypes, losses = pl.pallas_call(
        kernel,
        out_shape=(
            jax.ShapeDtypeStruct((B, K), F32),
            jax.ShapeDtypeStruct((B, K), F32),
            jax.ShapeDtypeStruct((1, B), F32),
        ),
        in_specs=[pl.BlockSpec(memory_space=pltpu.MemorySpace.HBM)] * 3,
        out_specs=(vmem,) * 3,
        scratch_shapes=[
            pltpu.VMEM((B, K), BF16), pltpu.VMEM((B, K), BF16), pltpu.VMEM((B, K), BF16),
            pltpu.VMEM((NY, B, K), BF16),
            pltpu.VMEM((NY, B, K), BF16),
            pltpu.VMEM((K, R), BF16),
            pltpu.VMEM((NP, B, K), BF16),
            pltpu.VMEM((R, C), F32),
            pltpu.VMEM((R, C), F32),
            pltpu.VMEM((R, C), F32),
            pltpu.VMEM((R, C), BF16),
            pltpu.VMEM((B, K), F32),
            pltpu.VMEM((B, K), F32),
            pltpu.VMEM((B, 128), F32),
            pltpu.VMEM((B, 128), F32),
            pltpu.VMEM((3, 8, 8, 128), F32),
            pltpu.VMEM((2, 8, 8, 128), F32),
            pltpu.VMEM((2, 8, 8, 128), F32),
            pltpu.VMEM((8, 24, 128), F32),
            pltpu.VMEM((8, 24, 128), F32),
            pltpu.VMEM((8, C), F32),
            pltpu.VMEM((8, 128), F32),
            pltpu.VMEM((24, 128), F32),
            pltpu.VMEM((B, C), BF16),
            pltpu.VMEM((2, B, 128), F32),
            *reduce_shapes(),
            *reduce_shapes(),
            pltpu.VMEM((B, K), F32),
            pltpu.VMEM((NP, K, B), F32),
            pltpu.VMEM((NX, K, B), F32),
            pltpu.VMEM((NX, K, B), F32),
            dma((3,)),
            dma((16,)), dma((16,)),
            dma((16,)), dma((16,)),
            dma((8,)), dma((8,)),
            dma((3, 8)), dma((3, 8)),
            dma((3, 8)), dma((3, 8)),
            dma((3, 8)), dma((3, 8)),
            dma((24,)), dma((24,)),
            dma((24,)), dma((24,)),
            dma((8,)), dma((8,)),
            dma((4,)), dma((4,)),
        ],
        compiler_params=pltpu.CompilerParams(
            collective_id=0, has_side_effects=True, vmem_limit_bytes=60 * 1024 * 1024
        ),
        name="dino_head",
    )(student_features, teacher_features, prototypes)
    return grad_features, grad_prototypes, losses.reshape(B)


def solution(mesh):
    in_specs = (P("dp", None), P("dp", None), P(("dp", "proto"), None))
    out_specs = (P("dp", None), P(("dp", "proto"), None), P("dp"))
    return jax.shard_map(shards, mesh=mesh, in_specs=in_specs, out_specs=out_specs, check_vma=False)
```

```python
import jax
import jax.numpy as jnp
from jax import lax
from jax.experimental import pallas as pl
from jax.experimental.pallas import tpu as pltpu
from jax.sharding import PartitionSpec as P

NY, NX, NC, NZ = 8, 4, 2, 8
NP = NX * NC
B = 128
K = 384
R = NY * B
C = NP * B
PIECE = B // NZ
CROPS = NY * NX * NC * B
TEACHER = 1.0 / 0.07
STUDENT = 1.0 / 0.1
EPS = 1e-06
MESH = pl.DeviceIdType.MESH
F32, BF16 = jnp.float32, jnp.bfloat16


def unit_rows(values):
    widened = values.astype(F32)
    inverse = lax.rsqrt(jnp.sum(widened * widened, axis=-1, keepdims=True) + EPS)
    return widened * inverse, inverse


def against_rows(a, b):
    return lax.dot_general(a, b, (((1,), (1,)), ((), ())), preferred_element_type=F32)


def project(unit, grad, inverse):
    return inverse * (grad - unit * jnp.sum(unit * grad, axis=1, keepdims=True))


def kernel(
    s_hbm, t_hbm, p_hbm, gf_ref, gp_ref, loss_ref,
    s_ref, t_ref, p_ref,
    t_all, s_all, s_turned, p_all, e_ref, l_ref, x_ref, g_ref, su_ref, pu_ref, sinv_ref, pinv_ref,
    colx, rowy, rowz, lasty, lastz, col_now, row_now, last_now,
    down_ref, us_ref, us_own, s_near_in, s_zfar, s_w, s_yfar, s_b, s_zn,
    ut_ref, ut_own, t_near_in, t_zfar, t_w, t_yfar, t_b, t_zn, gfb, v_ref, vsib, vx,
    ins, ts, tr, ss, sr, ps, pr, xs, xr, ys, yr, zs, zr, uss, usr, uts, utr, gs, gr, vs, vr,
):
    dp, z = lax.axis_index("dp"), lax.axis_index("proto")
    core = lax.rem(dp, NC)
    x = lax.rem(lax.div(dp, NC), NX)
    y = lax.div(dp, NC * NX)
    own = core * NX + x

    def at_y(other):
        return ((other * NX + x) * NC + core, z)

    def at_z(other):
        return (dp, other)

    def at_p(other):
        return ((y * NX + lax.rem(other, NX)) * NC + lax.div(other, NX), z)

    def ring(value, size):
        return lax.rem(value + size, size)

    def copy(src, dst, send, recv, device):
        return pltpu.make_async_remote_copy(
            src_ref=src, dst_ref=dst, send_sem=send, recv_sem=recv, device_id=device, device_id_type=MESH
        )

    def each(first, last, body):
        def step(i, carry):
            body(i)
            return carry

        lax.fori_loop(first, last, step, 0)

    loads = [
        pltpu.make_async_copy(far, here, ins.at[i])
        for i, (far, here) in enumerate(((t_hbm, t_ref), (p_hbm, p_ref), (s_hbm, s_ref)))
    ]
    for load in loads:
        load.start()

    barrier = pltpu.get_barrier_semaphore()

    def greet(q):
        for device in (at_y(ring(y + q, NY)), at_p(ring(own + q, NP)), at_z(ring(z + q, NZ))):
            pl.semaphore_signal(barrier, inc=1, device_id=device, device_id_type=MESH)

    each(1, 8, greet)

    for load in loads:
        load.wait()
    t_all[0] = unit_rows(t_ref[...])[0].astype(BF16)
    p_unit, p_inverse = unit_rows(p_ref[...])
    p_all[own] = p_unit.astype(BF16)
    pu_ref[...] = p_unit
    pinv_ref[...] = jnp.broadcast_to(p_inverse, (B, 128))
    s_unit, s_inverse = unit_rows(s_ref[...])
    s_all[0] = s_unit.astype(BF16)
    su_ref[...] = s_unit
    sinv_ref[...] = jnp.broadcast_to(s_inverse, (B, 128))
    pl.semaphore_wait(barrier, 21)

    log = []

    class Copies:
        def __init__(self, first, last, out, into):
            self.first, self.last, self.out, self.into = first, last, out, into
            self.left = set(range(first, last))

        def start(self):
            log.append(self)
            each(self.first, self.last, lambda i: self.out(i).start())

        def recv(self):
            self.left.clear()
            each(self.first, self.last, lambda i: self.into(i).wait_recv())

        def recv_one(self, i):
            if isinstance(i, int):
                self.left.discard(i)
            else:
                self.left.clear()
            self.into(i).wait_recv()

        def sent(self):
            each(self.first, self.last, lambda i: self.out(i).wait_send())

    def rows(who):
        return pl.ds(pl.multiple_of(who * PIECE, PIECE), PIECE)

    def crop_rows(d):
        return pl.ds(pl.multiple_of(d * B, B), B)

    def near_d(i):
        return ring((lax.div(i, 2) + 1) * (1 - 2 * lax.rem(i, 2)), NY)

    def over_z(make):
        return Copies(1, NZ, lambda j: make(j, z, ring(z + j, NZ)), lambda j: make(j, ring(z - j, NZ), ring(z + j, NZ)))

    def gather(ref, send, recv):
        def far_copy(d):
            return copy(
                ref.at[0, rows(z)], ref.at[d, rows(z)], send.at[d], recv.at[d], at_y(ring(y - d, NY))
            )

        def near_copy(i):
            d = near_d(i)
            return copy(ref.at[0], ref.at[d], send.at[d], recv.at[d], at_y(ring(y - d, NY)))

        def pass_copy(j, source, target):
            part = ref.at[pl.ds(3, 3), rows(source)]
            return copy(part, part, send.at[8 + j], recv.at[8 + j], at_z(target))

        return Copies(3, 6, far_copy, far_copy), Copies(0, 4, near_copy, near_copy), over_z(pass_copy)

    t_far, t_near, t_pass = gather(t_all, ts, tr)
    s_far, s_near, s_pass = gather(s_all, ss, sr)

    def x_copy(j, source, target):
        part = p_all.at[core * NX + source]
        return copy(part, part, ps.at[j], pr.at[j], at_p(core * NX + target))

    def over_x(make):
        return Copies(1, NX, lambda j: make(j, x, ring(x + j, NX)), lambda j: make(j, ring(x - j, NX), ring(x + j, NX)))

    def sib_copy(j, who):
        part = p_all.at[who * NX + ring(x - j, NX)]
        return copy(part, part, ps.at[4 + j], pr.at[4 + j], at_p((1 - core) * NX + x))

    p_x = over_x(x_copy)
    p_own = Copies(0, 1, lambda j: sib_copy(j, core), lambda j: sib_copy(j, 1 - core))
    p_passed = Copies(1, NX, lambda j: sib_copy(j, core), lambda j: sib_copy(j, 1 - core))

    p_x.start()
    t_far.start()
    t_near.start()
    p_own.start()
    s_far.start()
    t_far.recv()
    t_pass.start()
    p_x.recv()
    p_passed.start()
    s_far.recv()
    p_own.recv()
    p_passed.recv()
    s_near.start()

    def proto_pair(n):
        return p_all[2 * n : 2 * n + 2].reshape(2 * B, K)

    col_now[...] = jnp.zeros((8, C), F32)

    def teacher_block(d):
        block = t_all[d]
        for n in range(C // 256):
            lanes = slice(n * 256, (n + 1) * 256)
            expo = jnp.exp(against_rows(block, proto_pair(n)) * TEACHER)
            e_ref[crop_rows(d), lanes] = expo
            col_now[:, lanes] += jnp.sum(expo.reshape(B // 8, 8, 256), axis=0)

    teacher_block(0)

    def near_teacher(i):
        t_near.recv_one(i)
        teacher_block(near_d(i))

    each(0, 4, near_teacher)
    t_pass.recv()
    s_pass.start()
    each(3, 6, teacher_block)

    class Swap(Copies):
        def __init__(self, buf, send, recv, mine, at):
            def out(q):
                return copy(buf.at[mine], buf.at[mine], send.at[q], recv.at[mine], at(ring(mine + q, 8)))

            def into(q):
                source = ring(mine + q, 8)
                return copy(buf.at[source], buf.at[source], send.at[q], recv.at[source], at(source))

            super().__init__(1, 8, out, into)
            self.buf = buf

        def start(self):
            log.append(self)
            for q in (4, 3, 5, 2, 6, 1, 7):
                self.out(q).start()

        def total(self):
            self.left.clear()
            for q in (1, 7, 2, 6, 3, 5, 4):
                self.into(q).wait_recv()
            total = self.buf[0]
            for i in range(1, 8):
                total = total + self.buf[i]
            return total

    col_swap = [Swap(colx.at[it], xs.at[it], xr.at[it], own, at_p) for it in range(3)]
    y_swap = [Swap(rowy.at[it], ys.at[it], yr.at[it], y, at_y) for it in range(2)]
    z_swap = [Swap(rowz.at[it], zs.at[it], zr.at[it], z, at_z) for it in range(2)]
    last_y = Swap(lasty, ys.at[2], yr.at[2], y, at_y)
    last_z = Swap(lastz, zs.at[2], zr.at[2], z, at_z)

    def lane_rows(tile):
        return jnp.sum(tile.T, axis=0, keepdims=True)

    def down(vector):
        return jnp.broadcast_to(vector, (B, B)).T

    def lane_tile(k):
        return slice(k * B, (k + 1) * B)

    def times_protos(d):
        return jnp.dot(g_ref[crop_rows(d), :], p_all[...].reshape(C, K), preferred_element_type=F32)

    class Reduce:
        def __init__(self, u, u_own, near, zfar, w, yfar, b, zn, send, recv):
            self.bufs = u, u_own, near, zfar, w, yfar, b, zn

            def far_copy(j, source, target):
                part = u.at[pl.ds(3, 3), rows(target)]
                return copy(part, zfar.at[source], send.at[j], recv.at[j], at_z(target))

            def near_copy(i):
                d = near_d(i)
                return copy(u.at[d], near.at[i], send.at[8 + i], recv.at[8 + i], at_y(ring(y + d, NY)))

            def sum_copy(k):
                to = at_y(ring(y + 3 + k, NY))
                return copy(w.at[k], yfar.at[k], send.at[12 + k], recv.at[12 + k], to)

            def piece_copy(j, source, target):
                return copy(b.at[rows(target)], zn.at[source], send.at[16 + j], recv.at[16 + j], at_z(target))

            self.far, self.piece = over_z(far_copy), over_z(piece_copy)
            self.near, self.sum = Copies(0, 4, near_copy, near_copy), Copies(0, 3, sum_copy, sum_copy)

        def put(self, d, block):
            u, u_own = self.bufs[:2]
            if isinstance(d, int) and d == 0:
                u_own[...] = block
            else:
                u[d] = block.astype(BF16)

        def far_sums(self):
            u, _, _, zfar, w, _, _, _ = self.bufs
            self.far.recv()
            zfar[z] = u[pl.ds(3, 3), rows(z)]
            total = zfar[0].astype(F32)
            for i in range(1, NZ):
                total = total + zfar[i].astype(F32)
            w[...] = total
            self.sum.start()

        def near_sums(self):
            _, u_own, near, _, _, _, b, _ = self.bufs
            self.near.recv()
            b[...] = u_own[...] + sum(near[i].astype(F32) for i in range(4))
            self.piece.start()

        def result(self):
            _, _, _, _, _, yfar, b, zn = self.bufs
            self.piece.recv()
            self.sum.recv()
            zn[z] = b[rows(z)]
            total = yfar[0] + yfar[1] + yfar[2]
            for i in range(NZ):
                total = total + zn[i]
            return total

    s_reduce = Reduce(us_ref, us_own, s_near_in, s_zfar, s_w, s_yfar, s_b, s_zn, uss, usr)
    t_reduce = Reduce(ut_ref, ut_own, t_near_in, t_zfar, t_w, t_yfar, t_b, t_zn, uts, utr)

    def student_block(d):
        block = s_all[d]
        total = jnp.zeros((B, B), F32)
        for n in range(C // 256):
            lanes = slice(n * 256, (n + 1) * 256)
            logits = against_rows(block, proto_pair(n)) * STUDENT
            expo = jnp.exp(logits)
            l_ref[crop_rows(d), lanes] = logits
            x_ref[crop_rows(d), lanes] = expo
            g_ref[crop_rows(d), lanes] = expo.astype(BF16)
            total = total + expo[:, :B] + expo[:, B:]
        lasty[y, pl.ds(16 + ring(y + d, NY), 1), :] = lane_rows(total)
        s_turned[:, crop_rows(d)] = block.T
        s_reduce.put(d, times_protos(d))

    def near_student(i):
        s_near.recv_one(i)
        student_block(near_d(i))

    def weigh_rows(it):
        scale = col_now[:, :B]

        def block(d):
            total = jnp.zeros((B, B), F32)
            for k in range(NP):
                total = total + e_ref[crop_rows(d), lane_tile(k)] * scale[k : k + 1, :]
            rowy[it, y, pl.ds(ring(y + d, NY), 1), :] = lane_rows(total)

        each(0, NY, block)

    def weigh_columns(it):
        def block(d, totals):
            scale = down(row_now[pl.ds(ring(y + d, NY), 1), :])
            return tuple(
                totals[k]
                + jnp.sum((e_ref[crop_rows(d), lane_tile(k)] * scale).reshape(B // 8, 8, B), axis=0)
                for k in range(NP)
            )

        totals = lax.fori_loop(0, NY, block, (jnp.zeros((8, B), F32),) * NP)
        for k in range(NP):
            colx[it, own, k : k + 1, :] = jnp.sum(totals[k], axis=0, keepdims=True)

    for k in range(NP):
        colx[0, own, k : k + 1, :] = jnp.sum(col_now[:, lane_tile(k)], axis=0, keepdims=True)
    col_swap[0].start()
    student_block(0)
    col_now[:, :B] = 1.0 / col_swap[0].total()
    for it in range(2):
        weigh_rows(it)
        y_swap[it].start()
        if it == 0:
            near_student(0)
            near_student(1)
            near_student(2)
            near_student(3)
        rowz[it, z] = y_swap[it].total()
        z_swap[it].start()
        if it == 0:
            s_pass.recv()
            each(3, 6, student_block)
        row_now[...] = 1.0 / z_swap[it].total()
        if it == 0:
            s_reduce.far.start()
            s_reduce.near.start()
        else:
            s_reduce.far_sums()
            s_reduce.near_sums()
        weigh_columns(it + 1)
        col_swap[it + 1].start()
        col_now[:, :B] = 1.0 / col_swap[it + 1].total()

    def last_rows(d):
        scale = col_now[:, :B]
        total, mixed = jnp.zeros((B, B), F32), jnp.zeros((B, B), F32)
        for k in range(NP):
            scaled = e_ref[crop_rows(d), lane_tile(k)] * scale[k : k + 1, :]
            total = total + scaled
            mixed = mixed + scaled * l_ref[crop_rows(d), lane_tile(k)]
        lasty[y, pl.ds(ring(y + d, NY), 1), :] = lane_rows(total)
        lasty[y, pl.ds(8 + ring(y + d, NY), 1), :] = lane_rows(mixed)

    each(0, NY, last_rows)
    last_y.start()

    def teacher_grad(d):
        scale = col_now[:, :B]
        for k in range(NP):
            g_ref[crop_rows(d), lane_tile(k)] = (
                e_ref[crop_rows(d), lane_tile(k)] * scale[k : k + 1, :]
            ).astype(BF16)
        t_reduce.put(d, times_protos(d))

    each(3, 6, teacher_grad)
    t_reduce.far.start()

    def near_grad(i):
        teacher_grad(near_d(i))
        t_reduce.near.out(i).start()

    log.append(t_reduce.near)
    each(0, 4, near_grad)
    lastz[z] = last_y.total()
    last_z.start()
    teacher_grad(0)
    last_now[...] = last_z.total()
    row_total, mixed_total, student_total = last_now[0:8], last_now[8:16], last_now[16:24]
    row_now[...] = jnp.log(student_total) - mixed_total / row_total
    loss_ref[...] = row_now[pl.ds(y, 1), :]
    last_now[0:8] = 1.0 / row_total
    last_now[16:24] = 1.0 / student_total
    down_ref[0] = down(last_now[pl.ds(y, 1), :])
    down_ref[1] = down(last_now[pl.ds(16 + y, 1), :])

    def grad_block(d):
        b = ring(y + d, NY)
        scale = col_now[:, :B]
        row_scale, student_scale = down(last_now[pl.ds(b, 1), :]), down(last_now[pl.ds(16 + b, 1), :])
        for k in range(NP):
            target = e_ref[crop_rows(d), lane_tile(k)] * scale[k : k + 1, :] * row_scale
            g_ref[crop_rows(d), lane_tile(k)] = (
                x_ref[crop_rows(d), lane_tile(k)] * student_scale - target
            ).astype(BF16)

    each(0, NY, grad_block)

    def proto_grad(half):
        def pair(n):
            first = pl.multiple_of((half * 2 + n) * 256, 256)
            both = jnp.dot(s_turned[...], g_ref[:, pl.ds(first, 256)], preferred_element_type=F32)
            v_ref[half * NX + 2 * n] = both[:, :B]
            v_ref[half * NX + 2 * n + 1] = both[:, B:]

        each(0, 2, pair)

    def v_sib_copy(who):
        return copy(v_ref.at[pl.ds(who * NX, NX)], vsib, vs.at[0], vr.at[0], at_p((1 - core) * NX + x))

    def v_x_copy(j, source, target):
        return copy(
            v_ref.at[core * NX + target], vx.at[source], vs.at[j], vr.at[j], at_p(core * NX + target)
        )

    v_sib = Copies(0, 1, lambda i: v_sib_copy(1 - core), lambda i: v_sib_copy(1 - core))
    v_x = over_x(v_x_copy)

    proto_grad(1 - core)
    v_sib.start()
    proto_grad(core)

    v_sib.recv()

    def add_sibling(i):
        v_ref[core * NX + i] += vsib[i]

    each(0, NX, add_sibling)
    v_x.start()
    t_reduce.near_sums()
    t_reduce.far_sums()

    v_x.recv()
    vx[x] = v_ref[own]
    proto_sum = (vx[0] + vx[1] + vx[2] + vx[3]).T * (STUDENT / CROPS)
    gp_ref[...] = project(pu_ref[...], proto_sum, pinv_ref[:, 0:1])
    student_part = s_reduce.result() * down_ref[1, rows(z), 0:1]
    teacher_part = t_reduce.result() * down_ref[0, rows(z), 0:1]
    unit_grad = (student_part - teacher_part) * (STUDENT / CROPS)
    gfb[rows(z)] = project(su_ref[rows(z)], unit_grad, sinv_ref[rows(z), 0:1])

    def all_copy(j, source, target):
        part = gfb.at[rows(source)]
        return copy(part, part, gs.at[j], gr.at[j], at_z(target))

    every = over_z(all_copy)
    every.start()
    every.recv()
    gf_ref[...] = gfb[...]

    for group in log:
        group.sent()


def reduce_shapes():
    return [
        pltpu.VMEM((NY, B, K), BF16),
        pltpu.VMEM((B, K), F32),
        pltpu.VMEM((4, B, K), BF16),
        pltpu.VMEM((NZ, 3, PIECE, K), BF16),
        pltpu.VMEM((3, PIECE, K), F32),
        pltpu.VMEM((3, PIECE, K), F32),
        pltpu.VMEM((B, K), F32),
        pltpu.VMEM((NZ, PIECE, K), F32),
    ]


def shards(student_features, teacher_features, prototypes):
    vmem = pl.BlockSpec(memory_space=pltpu.VMEM)
    dma = pltpu.SemaphoreType.DMA
    grad_features, grad_prototypes, losses = pl.pallas_call(
        kernel,
        out_shape=(
            jax.ShapeDtypeStruct((B, K), F32),
            jax.ShapeDtypeStruct((B, K), F32),
            jax.ShapeDtypeStruct((1, B), F32),
        ),
        in_specs=[pl.BlockSpec(memory_space=pltpu.MemorySpace.HBM)] * 3,
        out_specs=(vmem,) * 3,
        scratch_shapes=[
            pltpu.VMEM((B, K), BF16), pltpu.VMEM((B, K), BF16), pltpu.VMEM((B, K), BF16),
            pltpu.VMEM((NY, B, K), BF16),
            pltpu.VMEM((NY, B, K), BF16),
            pltpu.VMEM((K, R), BF16),
            pltpu.VMEM((NP, B, K), BF16),
            pltpu.VMEM((R, C), F32),
            pltpu.VMEM((R, C), F32),
            pltpu.VMEM((R, C), F32),
            pltpu.VMEM((R, C), BF16),
            pltpu.VMEM((B, K), F32),
            pltpu.VMEM((B, K), F32),
            pltpu.VMEM((B, 128), F32),
            pltpu.VMEM((B, 128), F32),
            pltpu.VMEM((3, 8, 8, 128), F32),
            pltpu.VMEM((2, 8, 8, 128), F32),
            pltpu.VMEM((2, 8, 8, 128), F32),
            pltpu.VMEM((8, 24, 128), F32),
            pltpu.VMEM((8, 24, 128), F32),
            pltpu.VMEM((8, C), F32),
            pltpu.VMEM((8, 128), F32),
            pltpu.VMEM((24, 128), F32),
            pltpu.VMEM((2, B, 128), F32),
            *reduce_shapes(),
            *reduce_shapes(),
            pltpu.VMEM((B, K), F32),
            pltpu.VMEM((NP, K, B), F32),
            pltpu.VMEM((NX, K, B), F32),
            pltpu.VMEM((NX, K, B), F32),
            dma((3,)),
            dma((16,)), dma((16,)),
            dma((16,)), dma((16,)),
            dma((8,)), dma((8,)),
            dma((3, 8)), dma((3, 8)),
            dma((3, 8)), dma((3, 8)),
            dma((3, 8)), dma((3, 8)),
            dma((24,)), dma((24,)),
            dma((24,)), dma((24,)),
            dma((8,)), dma((8,)),
            dma((4,)), dma((4,)),
        ],
        compiler_params=pltpu.CompilerParams(
            collective_id=0, has_side_effects=True, vmem_limit_bytes=60 * 1024 * 1024
        ),
        name="dino_head",
    )(student_features, teacher_features, prototypes)
    return grad_features, grad_prototypes, losses.reshape(B)


def solution(mesh):
    in_specs = (P("dp", None), P("dp", None), P(("dp", "proto"), None))
    out_specs = (P("dp", None), P(("dp", "proto"), None), P("dp"))
    return jax.shard_map(shards, mesh=mesh, in_specs=in_specs, out_specs=out_specs, check_vma=False)
```

```python
import jax
import jax.numpy as jnp
from jax import lax
from jax.experimental import pallas as pl
from jax.experimental.pallas import tpu as pltpu
from jax.sharding import PartitionSpec as P

NY, NX, NC, NZ = 8, 4, 2, 8
NP = NX * NC
B = 128
K = 384
R = NY * B
C = NP * B
PIECE = B // NZ
CROPS = NY * NX * NC * B
TEACHER = 1.0 / 0.07
STUDENT = 1.0 / 0.1
EPS = 1e-06
MESH = pl.DeviceIdType.MESH
F32, BF16 = jnp.float32, jnp.bfloat16


def unit_rows(values):
    widened = values.astype(F32)
    inverse = lax.rsqrt(jnp.sum(widened * widened, axis=-1, keepdims=True) + EPS)
    return widened * inverse, inverse


def against_rows(a, b):
    return lax.dot_general(a, b, (((1,), (1,)), ((), ())), preferred_element_type=F32)


def project(unit, grad, inverse):
    return inverse * (grad - unit * jnp.sum(unit * grad, axis=1, keepdims=True))


def kernel(
    s_hbm, t_hbm, p_hbm, gf_ref, gp_ref, loss_ref,
    s_ref, t_ref, p_ref,
    t_all, s_all, s_turned, p_all, e_ref, l_ref, x_ref, g_ref, su_ref, pu_ref, sinv_ref, pinv_ref,
    colx, rowy, rowz, col_now, row_now, last_now,
    down_ref, us_ref, us_own, s_near_in, s_zfar, s_w, s_yfar, s_b, s_zn,
    ut_ref, ut_own, t_near_in, t_zfar, t_w, t_yfar, t_b, t_zn, gfb, v_ref, vsib, vx,
    ins, ts, tr, ss, sr, ps, pr, xs, xr, ys, yr, zs, zr, uss, usr, uts, utr, gs, gr, vs, vr,
):
    dp, z = lax.axis_index("dp"), lax.axis_index("proto")
    core = lax.rem(dp, NC)
    x = lax.rem(lax.div(dp, NC), NX)
    y = lax.div(dp, NC * NX)
    own = core * NX + x

    def at_y(other):
        return ((other * NX + x) * NC + core, z)

    def at_z(other):
        return (dp, other)

    def at_p(other):
        return ((y * NX + lax.rem(other, NX)) * NC + lax.div(other, NX), z)

    def ring(value, size):
        return lax.rem(value + size, size)

    def copy(src, dst, send, recv, device):
        return pltpu.make_async_remote_copy(
            src_ref=src, dst_ref=dst, send_sem=send, recv_sem=recv, device_id=device, device_id_type=MESH
        )

    def each(first, last, body, unroll=1):
        def step(i, carry):
            body(i)
            return carry

        lax.fori_loop(first, last, step, 0, unroll=unroll)

    loads = [
        pltpu.make_async_copy(far, here, ins.at[i])
        for i, (far, here) in enumerate(((t_hbm, t_ref), (p_hbm, p_ref), (s_hbm, s_ref)))
    ]
    for load in loads:
        load.start()

    barrier = pltpu.get_barrier_semaphore()

    def greet(q):
        for device in (at_y(ring(y + q, NY)), at_p(ring(own + q, NP)), at_z(ring(z + q, NZ))):
            pl.semaphore_signal(barrier, inc=1, device_id=device, device_id_type=MESH)

    each(1, 8, greet)

    for load in loads:
        load.wait()
    t_all[0] = unit_rows(t_ref[...])[0].astype(BF16)
    p_unit, p_inverse = unit_rows(p_ref[...])
    p_all[own] = p_unit.astype(BF16)
    pu_ref[...] = p_unit
    pinv_ref[...] = jnp.broadcast_to(p_inverse, (B, 128))
    s_unit, s_inverse = unit_rows(s_ref[...])
    s_all[0] = s_unit.astype(BF16)
    su_ref[...] = s_unit
    sinv_ref[...] = jnp.broadcast_to(s_inverse, (B, 128))
    pl.semaphore_wait(barrier, 21)

    log = []

    class Copies:
        def __init__(self, first, last, out, into):
            self.first, self.last, self.out, self.into = first, last, out, into
            self.left = set(range(first, last))

        def start(self):
            log.append(self)
            each(self.first, self.last, lambda i: self.out(i).start())

        def start_all(self):
            log.append(self)
            for i in range(self.first, self.last):
                self.out(i).start()

        def recv(self):
            self.left.clear()
            each(self.first, self.last, lambda i: self.into(i).wait_recv())

        def recv_one(self, i):
            if isinstance(i, int):
                self.left.discard(i)
            else:
                self.left.clear()
            self.into(i).wait_recv()

        def sent(self):
            for i in range(self.first, self.last):
                self.out(i).wait_send()

    def rows(who):
        return pl.ds(pl.multiple_of(who * PIECE, PIECE), PIECE)

    def crop_rows(d):
        return pl.ds(pl.multiple_of(d * B, B), B)

    def near_d(i):
        return ring((lax.div(i, 2) + 1) * (1 - 2 * lax.rem(i, 2)), NY)

    def over_z(make):
        return Copies(1, NZ, lambda j: make(j, z, ring(z + j, NZ)), lambda j: make(j, ring(z - j, NZ), ring(z + j, NZ)))

    def gather(ref, send, recv):
        def far_copy(d):
            return copy(
                ref.at[0, rows(z)], ref.at[d, rows(z)], send.at[d], recv.at[d], at_y(ring(y - d, NY))
            )

        def near_copy(i):
            d = near_d(i)
            return copy(ref.at[0], ref.at[d], send.at[d], recv.at[d], at_y(ring(y - d, NY)))

        def pass_copy(j, source, target):
            part = ref.at[pl.ds(3, 3), rows(source)]
            return copy(part, part, send.at[8 + j], recv.at[8 + j], at_z(target))

        return Copies(3, 6, far_copy, far_copy), Copies(0, 4, near_copy, near_copy), over_z(pass_copy)

    s_far, s_near, s_pass = gather(s_all, ss, sr)

    def step(k):
        def hand_on(i):
            side, half = i % 2, pl.ds(i // 2 * (B // 2), B // 2)
            there, here = (k, k - 1) if side == 0 else (NY - k, (NY + 1 - k) % NY)
            to = at_y(ring(y - 1, NY)) if side == 0 else at_y(ring(y + 1, NY))
            index = 4 * (k - 1) + i
            return copy(t_all.at[here, half], t_all.at[there, half], ts.at[index], tr.at[index], to)

        return Copies(0, 4, hand_on, hand_on)

    def t_piece_copy(i):
        part = (4, rows(z))
        return copy(t_all.at[0, rows(z)], t_all.at[part], ts.at[12], tr.at[12], at_y(ring(y + 4, NY)))

    def t_pass_copy(j, source, target):
        part = t_all.at[4, rows(source)]
        return copy(part, part, ts.at[12 + j], tr.at[12 + j], at_z(target))

    t_steps = [step(k) for k in (1, 2, 3)]
    t_piece, t_pass = Copies(0, 1, t_piece_copy, t_piece_copy), over_z(t_pass_copy)

    def x_copy(j, source, target):
        part = p_all.at[core * NX + source]
        return copy(part, part, ps.at[j], pr.at[j], at_p(core * NX + target))

    def over_x(make):
        return Copies(1, NX, lambda j: make(j, x, ring(x + j, NX)), lambda j: make(j, ring(x - j, NX), ring(x + j, NX)))

    def sib_copy(j, who):
        part = p_all.at[who * NX + ring(x - j, NX)]
        return copy(part, part, ps.at[4 + j], pr.at[4 + j], at_p((1 - core) * NX + x))

    p_x = over_x(x_copy)
    p_own = Copies(0, 1, lambda j: sib_copy(j, core), lambda j: sib_copy(j, 1 - core))
    p_passed = Copies(1, NX, lambda j: sib_copy(j, core), lambda j: sib_copy(j, 1 - core))

    t_piece.start()
    p_x.start()
    t_steps[0].start_all()
    p_own.start()
    for now, later in zip(t_steps, t_steps[1:]):
        log.append(later)
        for i in range(4):
            now.recv_one(i)
            later.out(i).start()
        if later is t_steps[1]:
            t_piece.recv()
            t_pass.start()
    s_far.start()
    p_x.recv()
    p_passed.start()
    p_own.recv()
    s_near.start()
    p_passed.recv()

    def proto_pair(n):
        return p_all[2 * n : 2 * n + 2].reshape(2 * B, K)

    col_now[...] = jnp.zeros((8, C), F32)

    def teacher_block(d):
        block = t_all[d]
        for n in range(C // 256):
            lanes = slice(n * 256, (n + 1) * 256)
            expo = jnp.exp(against_rows(block, proto_pair(n)) * TEACHER)
            e_ref[crop_rows(d), lanes] = expo
            col_now[:, lanes] += jnp.sum(expo.reshape(B // 8, 8, 256), axis=0)

    for d in (0, 1, 7, 2, 6):
        teacher_block(d)
    for i in range(4):
        t_steps[2].recv_one(i)
    for d in (3, 5):
        teacher_block(d)
    t_pass.recv()
    s_far.recv()
    s_pass.start()
    teacher_block(4)

    class Swap(Copies):
        def __init__(self, buf, send, recv, mine, at):
            def out(q):
                return copy(buf.at[mine], buf.at[mine], send.at[q], recv.at[mine], at(ring(mine + q, 8)))

            def into(q):
                source = ring(mine + q, 8)
                return copy(buf.at[source], buf.at[source], send.at[q], recv.at[source], at(source))

            super().__init__(1, 8, out, into)
            self.buf = buf

        def start(self):
            log.append(self)
            for q in (4, 3, 5, 2, 6, 1, 7):
                self.out(q).start()

        def total(self):
            self.left.clear()
            for q in (1, 7, 2, 6, 3, 5, 4):
                self.into(q).wait_recv()
            total = self.buf[0]
            for i in range(1, 8):
                total = total + self.buf[i]
            return total

    col_swap = [Swap(colx.at[it], xs.at[it], xr.at[it], own, at_p) for it in range(3)]
    y_swap = [Swap(rowy.at[it], ys.at[it], yr.at[it], y, at_y) for it in range(2)]
    z_swap = [Swap(rowz.at[it], zs.at[it], zr.at[it], z, at_z) for it in range(2)]
    last_y = Swap(rowy.at[2], ys.at[2], yr.at[2], y, at_y)
    last_z = Swap(rowz.at[2], zs.at[2], zr.at[2], z, at_z)
    student_y = Swap(rowy.at[3], ys.at[3], yr.at[3], y, at_y)
    student_z = Swap(rowz.at[3], zs.at[3], zr.at[3], z, at_z)
    mixed_y = Swap(rowy.at[4], ys.at[4], yr.at[4], y, at_y)
    mixed_z = Swap(rowz.at[4], zs.at[4], zr.at[4], z, at_z)

    def lane_rows(tile):
        return jnp.sum(tile.T, axis=0, keepdims=True)

    def down(vector):
        return jnp.broadcast_to(vector, (B, B)).T

    def lane_tile(k):
        return slice(k * B, (k + 1) * B)

    def times_protos(d):
        return jnp.dot(g_ref[crop_rows(d), :], p_all[...].reshape(C, K), preferred_element_type=F32)

    class Reduce:
        def __init__(self, u, u_own, near, zfar, w, yfar, b, zn, send, recv):
            self.bufs = u, u_own, near, zfar, w, yfar, b, zn

            def far_copy(j, source, target):
                part = u.at[pl.ds(3, 3), rows(target)]
                return copy(part, zfar.at[source], send.at[j], recv.at[j], at_z(target))

            def near_copy(i):
                d = near_d(i)
                return copy(u.at[d], near.at[i], send.at[8 + i], recv.at[8 + i], at_y(ring(y + d, NY)))

            def sum_copy(k):
                to = at_y(ring(y + 3 + k, NY))
                return copy(w.at[k], yfar.at[k], send.at[12 + k], recv.at[12 + k], to)

            def piece_copy(j, source, target):
                return copy(b.at[rows(target)], zn.at[source], send.at[16 + j], recv.at[16 + j], at_z(target))

            self.far, self.piece = over_z(far_copy), over_z(piece_copy)
            self.near, self.sum = Copies(0, 4, near_copy, near_copy), Copies(0, 3, sum_copy, sum_copy)

        def put(self, d, block):
            u, u_own = self.bufs[:2]
            if isinstance(d, int) and d == 0:
                u_own[...] = block
            else:
                u[d] = block.astype(BF16)

        def far_sums(self):
            u, _, _, zfar, w, _, _, _ = self.bufs
            self.far.recv()
            zfar[z] = u[pl.ds(3, 3), rows(z)]
            total = zfar[0].astype(F32)
            for i in range(1, NZ):
                total = total + zfar[i].astype(F32)
            w[...] = total
            self.sum.start()

        def near_sums(self):
            _, u_own, near, _, _, _, b, _ = self.bufs
            self.near.recv()
            b[...] = u_own[...] + sum(near[i].astype(F32) for i in range(4))
            self.piece.start()

        def result(self):
            _, _, _, _, _, yfar, b, zn = self.bufs
            self.piece.recv()
            self.sum.recv()
            zn[z] = b[rows(z)]
            total = yfar[0] + yfar[1] + yfar[2]
            for i in range(NZ):
                total = total + zn[i]
            return total

    s_reduce = Reduce(us_ref, us_own, s_near_in, s_zfar, s_w, s_yfar, s_b, s_zn, uss, usr)
    t_reduce = Reduce(ut_ref, ut_own, t_near_in, t_zfar, t_w, t_yfar, t_b, t_zn, uts, utr)

    def student_block(d):
        block = s_all[d]
        total = jnp.zeros((B, B), F32)
        for n in range(C // 256):
            lanes = slice(n * 256, (n + 1) * 256)
            logits = against_rows(block, proto_pair(n)) * STUDENT
            expo = jnp.exp(logits)
            l_ref[crop_rows(d), lanes] = logits
            x_ref[crop_rows(d), lanes] = expo
            g_ref[crop_rows(d), lanes] = expo.astype(BF16)
            total = total + expo[:, :B] + expo[:, B:]
        rowy[3, y, pl.ds(ring(y + d, NY), 1), :] = lane_rows(total)
        s_turned[:, crop_rows(d)] = block.T
        s_reduce.put(d, times_protos(d))

    def near_student(i):
        s_near.recv_one(i)
        student_block(near_d(i))

    def weigh_rows(it):
        scale = col_now[:, :B]

        def block(d):
            total = jnp.zeros((B, B), F32)
            for k in range(NP):
                total = total + e_ref[crop_rows(d), lane_tile(k)] * scale[k : k + 1, :]
            rowy[it, y, pl.ds(ring(y + d, NY), 1), :] = lane_rows(total)

        each(0, NY, block, 8)

    def weigh_columns(it):
        def block(d, totals):
            scale = down(row_now[pl.ds(ring(y + d, NY), 1), :])
            return tuple(
                totals[k]
                + jnp.sum((e_ref[crop_rows(d), lane_tile(k)] * scale).reshape(B // 8, 8, B), axis=0)
                for k in range(NP)
            )

        totals = lax.fori_loop(0, NY, block, (jnp.zeros((8, B), F32),) * NP, unroll=8)
        for k in range(NP):
            colx[it, own, k : k + 1, :] = jnp.sum(totals[k], axis=0, keepdims=True)

    for k in range(NP):
        colx[0, own, k : k + 1, :] = jnp.sum(col_now[:, lane_tile(k)], axis=0, keepdims=True)
    col_swap[0].start()
    student_block(0)
    col_now[:, :B] = 1.0 / col_swap[0].total()
    for it in range(2):
        weigh_rows(it)
        y_swap[it].start()
        if it == 0:
            near_student(0)
            near_student(1)
            near_student(2)
            near_student(3)
        rowz[it, z] = y_swap[it].total()
        z_swap[it].start()
        if it == 0:
            s_pass.recv()
            each(3, 6, student_block, 3)
        row_now[...] = 1.0 / z_swap[it].total()
        if it == 0:
            student_y.start()
            s_reduce.far.start()
            s_reduce.near.start()
        else:
            rowz[3, z] = student_y.total()
            student_z.start()
            s_reduce.far_sums()
            s_reduce.near_sums()
        weigh_columns(it + 1)
        col_swap[it + 1].start()
        col_now[:, :B] = 1.0 / col_swap[it + 1].total()

    def last_rows(d):
        scale = col_now[:, :B]
        total = jnp.zeros((B, B), F32)
        for k in range(NP):
            total = total + e_ref[crop_rows(d), lane_tile(k)] * scale[k : k + 1, :]
        rowy[2, y, pl.ds(ring(y + d, NY), 1), :] = lane_rows(total)

    def mixed_rows(d):
        scale = col_now[:, :B]
        mixed = jnp.zeros((B, B), F32)
        for k in range(NP):
            scaled = e_ref[crop_rows(d), lane_tile(k)] * scale[k : k + 1, :]
            mixed = mixed + scaled * l_ref[crop_rows(d), lane_tile(k)]
        rowy[4, y, pl.ds(ring(y + d, NY), 1), :] = lane_rows(mixed)

    each(0, NY, last_rows, 8)
    last_y.start()

    def teacher_grad(d):
        scale = col_now[:, :B]
        for k in range(NP):
            g_ref[crop_rows(d), lane_tile(k)] = (
                e_ref[crop_rows(d), lane_tile(k)] * scale[k : k + 1, :]
            ).astype(BF16)
        t_reduce.put(d, times_protos(d))

    each(3, 6, teacher_grad, 3)
    t_reduce.far.start()

    def near_grad(i):
        teacher_grad(near_d(i))
        t_reduce.near.out(i).start()

    log.append(t_reduce.near)
    each(0, 4, near_grad, 4)
    rowz[2, z] = last_y.total()
    last_z.start()
    teacher_grad(0)
    each(0, NY, mixed_rows, 8)
    mixed_y.start()
    last_now[8:16] = student_z.total()
    last_now[0:8] = last_z.total()
    last_now[16:24] = 1.0 / last_now[0:8]
    last_now[24:32] = 1.0 / last_now[8:16]
    down_ref[0] = down(last_now[pl.ds(16 + y, 1), :])
    down_ref[1] = down(last_now[pl.ds(24 + y, 1), :])

    def grad_block(d):
        b = ring(y + d, NY)
        scale = col_now[:, :B]
        row_scale, student_scale = down(last_now[pl.ds(16 + b, 1), :]), down(last_now[pl.ds(24 + b, 1), :])
        for k in range(NP):
            target = e_ref[crop_rows(d), lane_tile(k)] * scale[k : k + 1, :] * row_scale
            g_ref[crop_rows(d), lane_tile(k)] = (
                x_ref[crop_rows(d), lane_tile(k)] * student_scale - target
            ).astype(BF16)

    each(0, NY, grad_block, 8)

    def proto_grad(half):
        def pair(n):
            first = pl.multiple_of((half * 2 + n) * 256, 256)
            both = jnp.dot(s_turned[...], g_ref[:, pl.ds(first, 256)], preferred_element_type=F32)
            v_ref[half * NX + 2 * n] = both[:, :B]
            v_ref[half * NX + 2 * n + 1] = both[:, B:]

        each(0, 2, pair)

    def v_sib_copy(who):
        return copy(v_ref.at[pl.ds(who * NX, NX)], vsib, vs.at[0], vr.at[0], at_p((1 - core) * NX + x))

    def v_x_copy(j, source, target):
        return copy(
            v_ref.at[core * NX + target], vx.at[source], vs.at[j], vr.at[j], at_p(core * NX + target)
        )

    v_sib = Copies(0, 1, lambda i: v_sib_copy(1 - core), lambda i: v_sib_copy(1 - core))
    v_x = over_x(v_x_copy)

    proto_grad(1 - core)
    v_sib.start()
    t_reduce.near_sums()
    t_reduce.far_sums()
    rowz[4, z] = mixed_y.total()
    mixed_z.start()
    proto_grad(core)

    v_sib.recv()

    def add_sibling(i):
        v_ref[core * NX + i] += vsib[i]

    each(0, NX, add_sibling, 4)
    v_x.start()
    student_part = s_reduce.result() * down_ref[1, rows(z), 0:1]
    teacher_part = t_reduce.result() * down_ref[0, rows(z), 0:1]
    unit_grad = (student_part - teacher_part) * (STUDENT / CROPS)
    gfb[rows(z)] = project(su_ref[rows(z)], unit_grad, sinv_ref[rows(z), 0:1])

    def all_copy(j, source, target):
        part = gfb.at[rows(source)]
        return copy(part, part, gs.at[j], gr.at[j], at_z(target))

    every = over_z(all_copy)
    every.start()
    row_now[...] = jnp.log(last_now[8:16]) - mixed_z.total() * last_now[16:24]
    loss_ref[...] = row_now[pl.ds(y, 1), :]

    v_x.recv()
    vx[x] = v_ref[own]
    proto_sum = (vx[0] + vx[1] + vx[2] + vx[3]).T * (STUDENT / CROPS)
    gp_ref[...] = project(pu_ref[...], proto_sum, pinv_ref[:, 0:1])
    every.recv()
    gf_ref[...] = gfb[...]

    for group in log:
        group.sent()


def reduce_shapes():
    return [
        pltpu.VMEM((NY, B, K), BF16),
        pltpu.VMEM((B, K), F32),
        pltpu.VMEM((4, B, K), BF16),
        pltpu.VMEM((NZ, 3, PIECE, K), BF16),
        pltpu.VMEM((3, PIECE, K), F32),
        pltpu.VMEM((3, PIECE, K), F32),
        pltpu.VMEM((B, K), F32),
        pltpu.VMEM((NZ, PIECE, K), F32),
    ]


def shards(student_features, teacher_features, prototypes):
    vmem = pl.BlockSpec(memory_space=pltpu.VMEM)
    dma = pltpu.SemaphoreType.DMA
    grad_features, grad_prototypes, losses = pl.pallas_call(
        kernel,
        out_shape=(
            jax.ShapeDtypeStruct((B, K), F32),
            jax.ShapeDtypeStruct((B, K), F32),
            jax.ShapeDtypeStruct((1, B), F32),
        ),
        in_specs=[pl.BlockSpec(memory_space=pltpu.MemorySpace.HBM)] * 3,
        out_specs=(vmem,) * 3,
        scratch_shapes=[
            pltpu.VMEM((B, K), BF16), pltpu.VMEM((B, K), BF16), pltpu.VMEM((B, K), BF16),
            pltpu.VMEM((NY, B, K), BF16),
            pltpu.VMEM((NY, B, K), BF16),
            pltpu.VMEM((K, R), BF16),
            pltpu.VMEM((NP, B, K), BF16),
            pltpu.VMEM((R, C), F32),
            pltpu.VMEM((R, C), F32),
            pltpu.VMEM((R, C), F32),
            pltpu.VMEM((R, C), BF16),
            pltpu.VMEM((B, K), F32),
            pltpu.VMEM((B, K), F32),
            pltpu.VMEM((B, 128), F32),
            pltpu.VMEM((B, 128), F32),
            pltpu.VMEM((3, 8, 8, 128), F32),
            pltpu.VMEM((5, 8, 8, 128), F32),
            pltpu.VMEM((5, 8, 8, 128), F32),
            pltpu.VMEM((8, C), F32),
            pltpu.VMEM((8, 128), F32),
            pltpu.VMEM((32, 128), F32),
            pltpu.VMEM((2, B, 128), F32),
            *reduce_shapes(),
            *reduce_shapes(),
            pltpu.VMEM((B, K), F32),
            pltpu.VMEM((NP, K, B), F32),
            pltpu.VMEM((NX, K, B), F32),
            pltpu.VMEM((NX, K, B), F32),
            dma((3,)),
            dma((20,)), dma((20,)),
            dma((16,)), dma((16,)),
            dma((8,)), dma((8,)),
            dma((3, 8)), dma((3, 8)),
            dma((5, 8)), dma((5, 8)),
            dma((5, 8)), dma((5, 8)),
            dma((24,)), dma((24,)),
            dma((24,)), dma((24,)),
            dma((8,)), dma((8,)),
            dma((4,)), dma((4,)),
        ],
        compiler_params=pltpu.CompilerParams(
            collective_id=0, has_side_effects=True, vmem_limit_bytes=50 * 1024 * 1024
        ),
        name="dino_head",
    )(*(pltpu.with_memory_space_constraint(a, pltpu.MemorySpace.HBM) for a in (student_features, teacher_features, prototypes)))
    return grad_features, grad_prototypes, losses.reshape(B)


def solution(mesh):
    in_specs = (P("dp", None), P("dp", None), P(("dp", "proto"), None))
    out_specs = (P("dp", None), P(("dp", "proto"), None), P("dp"))
    return jax.shard_map(shards, mesh=mesh, in_specs=in_specs, out_specs=out_specs, check_vma=False)
```

```python
import jax
import jax.numpy as jnp
from jax import lax
from jax.experimental import pallas as pl
from jax.experimental.pallas import tpu as pltpu
from jax.sharding import PartitionSpec as P

NY, NX, NC, NZ = 8, 4, 2, 8
NP = NX * NC
B = 128
K = 384
R = NY * B
C = NP * B
PIECE = B // NZ
CROPS = NY * NX * NC * B
TEACHER = 1.0 / 0.07
STUDENT = 1.0 / 0.1
EPS = 1e-06
MESH = pl.DeviceIdType.MESH
F32, BF16 = jnp.float32, jnp.bfloat16


def unit_rows(values):
    widened = values.astype(F32)
    inverse = lax.rsqrt(jnp.sum(widened * widened, axis=-1, keepdims=True) + EPS)
    return widened * inverse, inverse


def against_rows(a, b):
    return lax.dot_general(a, b, (((1,), (1,)), ((), ())), preferred_element_type=F32)


def project(unit, grad, inverse):
    return inverse * (grad - unit * jnp.sum(unit * grad, axis=1, keepdims=True))


def kernel(
    s_hbm, t_hbm, p_hbm, gf_ref, gp_ref, loss_ref,
    s_ref, t_ref, p_ref,
    t_all, s_all, s_turned, p_all, e_ref, l_ref, x_ref, g_ref, su_ref, pu_ref, sinv_ref, pinv_ref,
    colx, rowy, rowz, col_now, row_now, last_now,
    down_ref, us_ref, us_own, s_near_in, s_zfar, s_w, s_yfar, s_b, s_zn,
    ut_ref, ut_own, t_near_in, t_zfar, t_w, t_yfar, t_b, t_zn, gfb, v_ref, vsib, vx,
    ins, ts, tr, ss, sr, ps, pr, xs, xr, ys, yr, zs, zr, uss, usr, uts, utr, gs, gr, vs, vr,
):
    dp, z = lax.axis_index("dp"), lax.axis_index("proto")
    core = lax.rem(dp, NC)
    x = lax.rem(lax.div(dp, NC), NX)
    y = lax.div(dp, NC * NX)
    own = core * NX + x

    def at_y(other):
        return ((other * NX + x) * NC + core, z)

    def at_z(other):
        return (dp, other)

    def at_p(other):
        return ((y * NX + lax.rem(other, NX)) * NC + lax.div(other, NX), z)

    def ring(value, size):
        return lax.rem(value + size, size)

    def copy(src, dst, send, recv, device):
        return pltpu.make_async_remote_copy(
            src_ref=src, dst_ref=dst, send_sem=send, recv_sem=recv, device_id=device, device_id_type=MESH
        )

    def each(first, last, body, unroll=1):
        def step(i, carry):
            body(i)
            return carry

        lax.fori_loop(first, last, step, 0, unroll=unroll)

    loads = [
        pltpu.make_async_copy(far, here, ins.at[i])
        for i, (far, here) in enumerate(((t_hbm, t_ref), (p_hbm, p_ref), (s_hbm, s_ref)))
    ]
    for load in loads:
        load.start()

    barrier = pltpu.get_barrier_semaphore()

    def greet(q):
        for device in (at_y(ring(y + q, NY)), at_p(ring(own + q, NP)), at_z(ring(z + q, NZ))):
            pl.semaphore_signal(barrier, inc=1, device_id=device, device_id_type=MESH)

    each(1, 8, greet)

    for load in loads:
        load.wait()
    t_all[0] = unit_rows(t_ref[...])[0].astype(BF16)
    p_unit, p_inverse = unit_rows(p_ref[...])
    p_all[own] = p_unit.astype(BF16)
    pu_ref[...] = p_unit
    pinv_ref[...] = jnp.broadcast_to(p_inverse, (B, 128))
    s_unit, s_inverse = unit_rows(s_ref[...])
    s_all[0] = s_unit.astype(BF16)
    su_ref[...] = s_unit
    sinv_ref[...] = jnp.broadcast_to(s_inverse, (B, 128))
    pl.semaphore_wait(barrier, 21)

    log = []

    class Copies:
        def __init__(self, first, last, out, into):
            self.first, self.last, self.out, self.into = first, last, out, into
            self.left = set(range(first, last))

        def start(self):
            log.append(self)
            each(self.first, self.last, lambda i: self.out(i).start())

        def start_all(self):
            log.append(self)
            for i in range(self.first, self.last):
                self.out(i).start()

        def recv(self):
            self.left.clear()
            each(self.first, self.last, lambda i: self.into(i).wait_recv())

        def recv_one(self, i):
            if isinstance(i, int):
                self.left.discard(i)
            else:
                self.left.clear()
            self.into(i).wait_recv()

        def sent(self):
            for i in range(self.first, self.last):
                self.out(i).wait_send()

    def rows(who):
        return pl.ds(pl.multiple_of(who * PIECE, PIECE), PIECE)

    def crop_rows(d):
        return pl.ds(pl.multiple_of(d * B, B), B)

    def near_d(i):
        return ring((lax.div(i, 2) + 1) * (1 - 2 * lax.rem(i, 2)), NY)

    def over_z(make):
        return Copies(1, NZ, lambda j: make(j, z, ring(z + j, NZ)), lambda j: make(j, ring(z - j, NZ), ring(z + j, NZ)))

    def gather(ref, send, recv):
        def far_copy(d):
            return copy(
                ref.at[0, rows(z)], ref.at[d, rows(z)], send.at[d], recv.at[d], at_y(ring(y - d, NY))
            )

        def near_copy(i):
            d = near_d(i)
            return copy(ref.at[0], ref.at[d], send.at[d], recv.at[d], at_y(ring(y - d, NY)))

        def pass_copy(j, source, target):
            part = ref.at[pl.ds(3, 3), rows(source)]
            return copy(part, part, send.at[8 + j], recv.at[8 + j], at_z(target))

        return Copies(3, 6, far_copy, far_copy), Copies(0, 4, near_copy, near_copy), over_z(pass_copy)

    s_far, s_near, s_pass = gather(s_all, ss, sr)

    def step(k):
        def hand_on(i):
            side, half = i % 2, pl.ds(i // 2 * (B // 2), B // 2)
            there, here = (k, k - 1) if side == 0 else (NY - k, (NY + 1 - k) % NY)
            to = at_y(ring(y - 1, NY)) if side == 0 else at_y(ring(y + 1, NY))
            index = 4 * (k - 1) + i
            return copy(t_all.at[here, half], t_all.at[there, half], ts.at[index], tr.at[index], to)

        return Copies(0, 4, hand_on, hand_on)

    def t_piece_copy(i):
        part = (4, rows(z))
        return copy(t_all.at[0, rows(z)], t_all.at[part], ts.at[12], tr.at[12], at_y(ring(y + 4, NY)))

    def t_pass_copy(j, source, target):
        part = t_all.at[4, rows(source)]
        return copy(part, part, ts.at[12 + j], tr.at[12 + j], at_z(target))

    t_steps = [step(k) for k in (1, 2, 3)]
    t_piece, t_pass = Copies(0, 1, t_piece_copy, t_piece_copy), over_z(t_pass_copy)

    def x_copy(j, source, target):
        part = p_all.at[core * NX + source]
        return copy(part, part, ps.at[j], pr.at[j], at_p(core * NX + target))

    def over_x(make):
        return Copies(1, NX, lambda j: make(j, x, ring(x + j, NX)), lambda j: make(j, ring(x - j, NX), ring(x + j, NX)))

    def sib_copy(j, who):
        part = p_all.at[who * NX + ring(x - j, NX)]
        return copy(part, part, ps.at[4 + j], pr.at[4 + j], at_p((1 - core) * NX + x))

    p_x = over_x(x_copy)
    p_own = Copies(0, 1, lambda j: sib_copy(j, core), lambda j: sib_copy(j, 1 - core))
    p_passed = Copies(1, NX, lambda j: sib_copy(j, core), lambda j: sib_copy(j, 1 - core))

    t_piece.start()
    p_x.start()
    t_steps[0].start_all()
    p_own.start()
    for now, later in zip(t_steps, t_steps[1:]):
        log.append(later)
        for i in range(4):
            now.recv_one(i)
            later.out(i).start()
        if later is t_steps[1]:
            s_far.start()
            t_piece.recv()
            t_pass.start()
    p_x.recv()
    p_passed.start()
    p_own.recv()
    s_far.recv()
    s_pass.start()
    s_near.start()
    p_passed.recv()

    def proto_pair(n):
        return p_all[2 * n : 2 * n + 2].reshape(2 * B, K)

    col_now[...] = jnp.zeros((8, C), F32)

    def teacher_block(d):
        block = t_all[d]
        for n in range(C // 256):
            lanes = slice(n * 256, (n + 1) * 256)
            expo = jnp.exp(against_rows(block, proto_pair(n)) * TEACHER)
            e_ref[crop_rows(d), lanes] = expo
            col_now[:, lanes] += jnp.sum(expo.reshape(B // 8, 8, 256), axis=0)

    for d in (0, 1, 7, 2, 6):
        teacher_block(d)
    for i in range(4):
        t_steps[2].recv_one(i)
    for d in (3, 5):
        teacher_block(d)
    t_pass.recv()
    teacher_block(4)

    class Swap(Copies):
        def __init__(self, buf, send, recv, mine, at):
            def out(q):
                return copy(buf.at[mine], buf.at[mine], send.at[q], recv.at[mine], at(ring(mine + q, 8)))

            def into(q):
                source = ring(mine + q, 8)
                return copy(buf.at[source], buf.at[source], send.at[q], recv.at[source], at(source))

            super().__init__(1, 8, out, into)
            self.buf = buf

        def start(self):
            log.append(self)
            for q in (4, 3, 5, 2, 6, 1, 7):
                self.out(q).start()

        def total(self):
            self.left.clear()
            for q in (1, 7, 2, 6, 3, 5, 4):
                self.into(q).wait_recv()
            total = self.buf[0]
            for i in range(1, 8):
                total = total + self.buf[i]
            return total

    col_swap = [Swap(colx.at[it], xs.at[it], xr.at[it], own, at_p) for it in range(3)]
    y_swap = [Swap(rowy.at[it], ys.at[it], yr.at[it], y, at_y) for it in range(2)]
    z_swap = [Swap(rowz.at[it], zs.at[it], zr.at[it], z, at_z) for it in range(2)]
    last_y = Swap(rowy.at[2], ys.at[2], yr.at[2], y, at_y)
    last_z = Swap(rowz.at[2], zs.at[2], zr.at[2], z, at_z)
    student_y = Swap(rowy.at[3], ys.at[3], yr.at[3], y, at_y)
    student_z = Swap(rowz.at[3], zs.at[3], zr.at[3], z, at_z)
    mixed_y = Swap(rowy.at[4], ys.at[4], yr.at[4], y, at_y)
    mixed_z = Swap(rowz.at[4], zs.at[4], zr.at[4], z, at_z)

    def lane_rows(tile):
        return jnp.sum(tile.T, axis=0, keepdims=True)

    def down(vector):
        return jnp.broadcast_to(vector, (B, B)).T

    def lane_tile(k):
        return slice(k * B, (k + 1) * B)

    def times_protos(d):
        return jnp.dot(g_ref[crop_rows(d), :], p_all[...].reshape(C, K), preferred_element_type=F32)

    class Reduce:
        def __init__(self, u, u_own, near, zfar, w, yfar, b, zn, send, recv):
            self.bufs = u, u_own, near, zfar, w, yfar, b, zn

            def far_copy(j, source, target):
                part = u.at[pl.ds(3, 3), rows(target)]
                return copy(part, zfar.at[source], send.at[j], recv.at[j], at_z(target))

            def near_copy(i):
                d = near_d(i)
                return copy(u.at[d], near.at[i], send.at[8 + i], recv.at[8 + i], at_y(ring(y + d, NY)))

            def sum_copy(k):
                to = at_y(ring(y + 3 + k, NY))
                return copy(w.at[k], yfar.at[k], send.at[12 + k], recv.at[12 + k], to)

            def piece_copy(j, source, target):
                return copy(b.at[rows(target)], zn.at[source], send.at[16 + j], recv.at[16 + j], at_z(target))

            self.far, self.piece = over_z(far_copy), over_z(piece_copy)
            self.near, self.sum = Copies(0, 4, near_copy, near_copy), Copies(0, 3, sum_copy, sum_copy)

        def put(self, d, block):
            u, u_own = self.bufs[:2]
            if isinstance(d, int) and d == 0:
                u_own[...] = block
            else:
                u[d] = block.astype(BF16)

        def far_sums(self):
            u, _, _, zfar, w, _, _, _ = self.bufs
            self.far.recv()
            zfar[z] = u[pl.ds(3, 3), rows(z)]
            total = zfar[0].astype(F32)
            for i in range(1, NZ):
                total = total + zfar[i].astype(F32)
            w[...] = total
            self.sum.start()

        def near_sums(self):
            _, u_own, near, _, _, _, b, _ = self.bufs
            self.near.recv()
            b[...] = u_own[...] + sum(near[i].astype(F32) for i in range(4))
            self.piece.start()

        def result(self):
            _, _, _, _, _, yfar, b, zn = self.bufs
            self.piece.recv()
            self.sum.recv()
            zn[z] = b[rows(z)]
            total = yfar[0] + yfar[1] + yfar[2]
            for i in range(NZ):
                total = total + zn[i]
            return total

    s_reduce = Reduce(us_ref, us_own, s_near_in, s_zfar, s_w, s_yfar, s_b, s_zn, uss, usr)
    t_reduce = Reduce(ut_ref, ut_own, t_near_in, t_zfar, t_w, t_yfar, t_b, t_zn, uts, utr)

    def student_block(d):
        block = s_all[d]
        total = jnp.zeros((B, B), F32)
        for n in range(C // 256):
            lanes = slice(n * 256, (n + 1) * 256)
            logits = against_rows(block, proto_pair(n)) * STUDENT
            expo = jnp.exp(logits)
            l_ref[crop_rows(d), lanes] = logits
            x_ref[crop_rows(d), lanes] = expo
            g_ref[crop_rows(d), lanes] = expo.astype(BF16)
            total = total + expo[:, :B] + expo[:, B:]
        rowy[3, y, pl.ds(ring(y + d, NY), 1), :] = lane_rows(total)
        s_turned[:, crop_rows(d)] = block.T
        s_reduce.put(d, times_protos(d))

    def near_student(i):
        s_near.recv_one(i)
        student_block(near_d(i))

    def weigh_rows(it):
        scale = col_now[:, :B]

        def block(d):
            total = jnp.zeros((B, B), F32)
            for k in range(NP):
                total = total + e_ref[crop_rows(d), lane_tile(k)] * scale[k : k + 1, :]
            rowy[it, y, pl.ds(ring(y + d, NY), 1), :] = lane_rows(total)

        each(0, NY, block, 8)

    def weigh_columns(it):
        def block(d, totals):
            scale = down(row_now[pl.ds(ring(y + d, NY), 1), :])
            return tuple(
                totals[k]
                + jnp.sum((e_ref[crop_rows(d), lane_tile(k)] * scale).reshape(B // 8, 8, B), axis=0)
                for k in range(NP)
            )

        totals = lax.fori_loop(0, NY, block, (jnp.zeros((8, B), F32),) * NP, unroll=8)
        for k in range(NP):
            colx[it, own, k : k + 1, :] = jnp.sum(totals[k], axis=0, keepdims=True)

    for k in range(NP):
        colx[0, own, k : k + 1, :] = jnp.sum(col_now[:, lane_tile(k)], axis=0, keepdims=True)
    col_swap[0].start()
    student_block(0)
    col_now[:, :B] = 1.0 / col_swap[0].total()
    for it in range(2):
        weigh_rows(it)
        y_swap[it].start()
        if it == 0:
            near_student(0)
            near_student(1)
            near_student(2)
            near_student(3)
        rowz[it, z] = y_swap[it].total()
        z_swap[it].start()
        if it == 0:
            s_reduce.near.start()
        if it == 0:
            s_pass.recv()
            each(3, 6, student_block, 3)
        row_now[...] = 1.0 / z_swap[it].total()
        if it == 0:
            student_y.start()
            s_reduce.far.start()
        else:
            rowz[3, z] = student_y.total()
            student_z.start()
            s_reduce.far_sums()
            s_reduce.near_sums()
        weigh_columns(it + 1)
        col_swap[it + 1].start()
        col_now[:, :B] = 1.0 / col_swap[it + 1].total()

    def last_rows(d):
        scale = col_now[:, :B]
        total = jnp.zeros((B, B), F32)
        for k in range(NP):
            total = total + e_ref[crop_rows(d), lane_tile(k)] * scale[k : k + 1, :]
        rowy[2, y, pl.ds(ring(y + d, NY), 1), :] = lane_rows(total)

    def mixed_rows(d):
        scale = col_now[:, :B]
        mixed = jnp.zeros((B, B), F32)
        for k in range(NP):
            scaled = e_ref[crop_rows(d), lane_tile(k)] * scale[k : k + 1, :]
            mixed = mixed + scaled * l_ref[crop_rows(d), lane_tile(k)]
        rowy[4, y, pl.ds(ring(y + d, NY), 1), :] = lane_rows(mixed)

    each(0, NY, last_rows, 8)
    last_y.start()

    def teacher_grad(d):
        scale = col_now[:, :B]
        for k in range(NP):
            g_ref[crop_rows(d), lane_tile(k)] = (
                e_ref[crop_rows(d), lane_tile(k)] * scale[k : k + 1, :]
            ).astype(BF16)
        t_reduce.put(d, times_protos(d))

    each(3, 6, teacher_grad, 3)
    t_reduce.far.start()

    def near_grad(i):
        teacher_grad(near_d(i))
        t_reduce.near.out(i).start()

    log.append(t_reduce.near)
    each(0, 4, near_grad, 4)
    rowz[2, z] = last_y.total()
    last_z.start()
    teacher_grad(0)
    each(0, NY, mixed_rows, 8)
    mixed_y.start()
    last_now[8:16] = student_z.total()
    last_now[0:8] = last_z.total()
    last_now[16:24] = 1.0 / last_now[0:8]
    last_now[24:32] = 1.0 / last_now[8:16]
    down_ref[0] = down(last_now[pl.ds(16 + y, 1), :])
    down_ref[1] = down(last_now[pl.ds(24 + y, 1), :])

    def grad_block(d):
        b = ring(y + d, NY)
        scale = col_now[:, :B]
        row_scale, student_scale = down(last_now[pl.ds(16 + b, 1), :]), down(last_now[pl.ds(24 + b, 1), :])
        for k in range(NP):
            target = e_ref[crop_rows(d), lane_tile(k)] * scale[k : k + 1, :] * row_scale
            g_ref[crop_rows(d), lane_tile(k)] = (
                x_ref[crop_rows(d), lane_tile(k)] * student_scale - target
            ).astype(BF16)

    each(0, NY, grad_block, 8)

    def proto_grad(half):
        def pair(n):
            first = pl.multiple_of((half * 2 + n) * 256, 256)
            both = jnp.dot(s_turned[...], g_ref[:, pl.ds(first, 256)], preferred_element_type=F32)
            v_ref[half * NX + 2 * n] = both[:, :B]
            v_ref[half * NX + 2 * n + 1] = both[:, B:]

        each(0, 2, pair)

    def v_sib_copy(who):
        return copy(v_ref.at[pl.ds(who * NX, NX)], vsib, vs.at[0], vr.at[0], at_p((1 - core) * NX + x))

    def v_x_copy(j, source, target):
        return copy(
            v_ref.at[core * NX + target], vx.at[source], vs.at[j], vr.at[j], at_p(core * NX + target)
        )

    v_sib = Copies(0, 1, lambda i: v_sib_copy(1 - core), lambda i: v_sib_copy(1 - core))
    v_x = over_x(v_x_copy)

    proto_grad(1 - core)
    v_sib.start()
    t_reduce.near_sums()
    t_reduce.far_sums()
    rowz[4, z] = mixed_y.total()
    mixed_z.start()
    proto_grad(core)

    v_sib.recv()

    def add_sibling(i):
        v_ref[core * NX + i] += vsib[i]

    each(0, NX, add_sibling, 4)
    v_x.start()
    student_part = s_reduce.result() * down_ref[1, rows(z), 0:1]
    teacher_part = t_reduce.result() * down_ref[0, rows(z), 0:1]
    unit_grad = (student_part - teacher_part) * (STUDENT / CROPS)
    gfb[rows(z)] = project(su_ref[rows(z)], unit_grad, sinv_ref[rows(z), 0:1])

    def all_copy(j, source, target):
        part = gfb.at[rows(source)]
        return copy(part, part, gs.at[j], gr.at[j], at_z(target))

    every = over_z(all_copy)
    every.start()
    row_now[...] = jnp.log(last_now[8:16]) - mixed_z.total() * last_now[16:24]
    loss_ref[...] = row_now[pl.ds(y, 1), :]

    v_x.recv()
    vx[x] = v_ref[own]
    proto_sum = (vx[0] + vx[1] + vx[2] + vx[3]).T * (STUDENT / CROPS)
    gp_ref[...] = project(pu_ref[...], proto_sum, pinv_ref[:, 0:1])
    every.recv()
    gf_ref[...] = gfb[...]

    for group in log:
        group.sent()


def reduce_shapes():
    return [
        pltpu.VMEM((NY, B, K), BF16),
        pltpu.VMEM((B, K), F32),
        pltpu.VMEM((4, B, K), BF16),
        pltpu.VMEM((NZ, 3, PIECE, K), BF16),
        pltpu.VMEM((3, PIECE, K), F32),
        pltpu.VMEM((3, PIECE, K), F32),
        pltpu.VMEM((B, K), F32),
        pltpu.VMEM((NZ, PIECE, K), F32),
    ]


def shards(student_features, teacher_features, prototypes):
    vmem = pl.BlockSpec(memory_space=pltpu.VMEM)
    dma = pltpu.SemaphoreType.DMA
    grad_features, grad_prototypes, losses = pl.pallas_call(
        kernel,
        out_shape=(
            jax.ShapeDtypeStruct((B, K), F32),
            jax.ShapeDtypeStruct((B, K), F32),
            jax.ShapeDtypeStruct((1, B), F32),
        ),
        in_specs=[pl.BlockSpec(memory_space=pltpu.MemorySpace.HBM)] * 3,
        out_specs=(vmem,) * 3,
        scratch_shapes=[
            pltpu.VMEM((B, K), BF16), pltpu.VMEM((B, K), BF16), pltpu.VMEM((B, K), BF16),
            pltpu.VMEM((NY, B, K), BF16),
            pltpu.VMEM((NY, B, K), BF16),
            pltpu.VMEM((K, R), BF16),
            pltpu.VMEM((NP, B, K), BF16),
            pltpu.VMEM((R, C), F32),
            pltpu.VMEM((R, C), F32),
            pltpu.VMEM((R, C), F32),
            pltpu.VMEM((R, C), BF16),
            pltpu.VMEM((B, K), F32),
            pltpu.VMEM((B, K), F32),
            pltpu.VMEM((B, 128), F32),
            pltpu.VMEM((B, 128), F32),
            pltpu.VMEM((3, 8, 8, 128), F32),
            pltpu.VMEM((5, 8, 8, 128), F32),
            pltpu.VMEM((5, 8, 8, 128), F32),
            pltpu.VMEM((8, C), F32),
            pltpu.VMEM((8, 128), F32),
            pltpu.VMEM((32, 128), F32),
            pltpu.VMEM((2, B, 128), F32),
            *reduce_shapes(),
            *reduce_shapes(),
            pltpu.VMEM((B, K), F32),
            pltpu.VMEM((NP, K, B), F32),
            pltpu.VMEM((NX, K, B), F32),
            pltpu.VMEM((NX, K, B), F32),
            dma((3,)),
            dma((20,)), dma((20,)),
            dma((16,)), dma((16,)),
            dma((8,)), dma((8,)),
            dma((3, 8)), dma((3, 8)),
            dma((5, 8)), dma((5, 8)),
            dma((5, 8)), dma((5, 8)),
            dma((24,)), dma((24,)),
            dma((24,)), dma((24,)),
            dma((8,)), dma((8,)),
            dma((4,)), dma((4,)),
        ],
        compiler_params=pltpu.CompilerParams(
            collective_id=0, has_side_effects=True, vmem_limit_bytes=50 * 1024 * 1024
        ),
        name="dino_head",
    )(*(pltpu.with_memory_space_constraint(a, pltpu.MemorySpace.HBM) for a in (student_features, teacher_features, prototypes)))
    return grad_features, grad_prototypes, losses.reshape(B)


def solution(mesh):
    in_specs = (P("dp", None), P("dp", None), P(("dp", "proto"), None))
    out_specs = (P("dp", None), P(("dp", "proto"), None), P("dp"))
    return jax.shard_map(shards, mesh=mesh, in_specs=in_specs, out_specs=out_specs, check_vma=False)
```

```python
import jax
import jax.numpy as jnp
from jax import lax
from jax.experimental import pallas as pl
from jax.experimental.pallas import tpu as pltpu
from jax.sharding import PartitionSpec as P

NY, NX, NC, NZ = 8, 4, 2, 8
NP = NX * NC
B = 128
K = 384
R = NY * B
C = NP * B
PIECE = B // NZ
CROPS = NY * NX * NC * B
TEACHER = 1.0 / 0.07
STUDENT = 1.0 / 0.1
EPS = 1e-06
MESH = pl.DeviceIdType.MESH
F32, BF16 = jnp.float32, jnp.bfloat16


def unit_rows(values):
    widened = values.astype(F32)
    inverse = lax.rsqrt(jnp.sum(widened * widened, axis=-1, keepdims=True) + EPS)
    return widened * inverse, inverse


def against_rows(a, b):
    return lax.dot_general(a, b, (((1,), (1,)), ((), ())), preferred_element_type=F32)


def project(unit, grad, inverse):
    return inverse * (grad - unit * jnp.sum(unit * grad, axis=1, keepdims=True))


def kernel(
    s_hbm, t_hbm, p_hbm, gf_ref, gp_ref, loss_ref,
    s_ref, t_ref, p_ref,
    t_all, s_all, s_turned, p_all, e_ref, l_ref, x_ref, g_ref, su_ref, pu_ref, sinv_ref, pinv_ref,
    colx, rowy, rowz, col_now, row_now, last_now,
    down_ref, us_ref, us_own, s_near_in, s_zfar, s_w, s_yfar, s_b, s_b16, s_zn,
    ut_ref, ut_own, t_near_in, t_zfar, t_w, t_yfar, t_b, t_b16, t_zn, gfb, v_ref, vsib, v_out, vx,
    ins, ts, tr, ss, sr, ps, pr, xs, xr, ys, yr, zs, zr, uss, usr, uts, utr, gs, gr, vs, vr,
):
    dp, z = lax.axis_index("dp"), lax.axis_index("proto")
    core = lax.rem(dp, NC)
    x = lax.rem(lax.div(dp, NC), NX)
    y = lax.div(dp, NC * NX)
    own = core * NX + x

    def at_y(other):
        return ((other * NX + x) * NC + core, z)

    def at_z(other):
        return (dp, other)

    def at_p(other):
        return ((y * NX + lax.rem(other, NX)) * NC + lax.div(other, NX), z)

    def ring(value, size):
        return lax.rem(value + size, size)

    def copy(src, dst, send, recv, device):
        return pltpu.make_async_remote_copy(
            src_ref=src, dst_ref=dst, send_sem=send, recv_sem=recv, device_id=device, device_id_type=MESH
        )

    def each(first, last, body, unroll=1):
        def step(i, carry):
            body(i)
            return carry

        lax.fori_loop(first, last, step, 0, unroll=unroll)

    loads = [
        pltpu.make_async_copy(far, here, ins.at[i])
        for i, (far, here) in enumerate(((t_hbm, t_ref), (p_hbm, p_ref), (s_hbm, s_ref)))
    ]
    for load in loads:
        load.start()

    barrier = pltpu.get_barrier_semaphore()

    def greet(q):
        for device in (at_y(ring(y + q, NY)), at_p(ring(own + q, NP)), at_z(ring(z + q, NZ))):
            pl.semaphore_signal(barrier, inc=1, device_id=device, device_id_type=MESH)

    each(1, 8, greet)

    for load in loads:
        load.wait()
    t_all[0] = unit_rows(t_ref[...])[0].astype(BF16)
    p_unit, p_inverse = unit_rows(p_ref[...])
    p_all[own] = p_unit.astype(BF16)
    pu_ref[...] = p_unit
    pinv_ref[...] = jnp.broadcast_to(p_inverse, (B, 128))
    s_unit, s_inverse = unit_rows(s_ref[...])
    s_all[0] = s_unit.astype(BF16)
    su_ref[...] = s_unit
    sinv_ref[...] = jnp.broadcast_to(s_inverse, (B, 128))
    pl.semaphore_wait(barrier, 21)

    log = []

    class Copies:
        def __init__(self, first, last, out, into):
            self.first, self.last, self.out, self.into = first, last, out, into
            self.left = set(range(first, last))

        def start(self):
            log.append(self)
            each(self.first, self.last, lambda i: self.out(i).start())

        def start_all(self):
            log.append(self)
            for i in range(self.first, self.last):
                self.out(i).start()

        def recv(self):
            self.left.clear()
            each(self.first, self.last, lambda i: self.into(i).wait_recv())

        def recv_one(self, i):
            if isinstance(i, int):
                self.left.discard(i)
            else:
                self.left.clear()
            self.into(i).wait_recv()

        def sent(self):
            for i in range(self.first, self.last):
                self.out(i).wait_send()

    def rows(who):
        return pl.ds(pl.multiple_of(who * PIECE, PIECE), PIECE)

    def crop_rows(d):
        return pl.ds(pl.multiple_of(d * B, B), B)

    def near_d(i):
        return ring((lax.div(i, 2) + 1) * (1 - 2 * lax.rem(i, 2)), NY)

    def over_z(make):
        return Copies(1, NZ, lambda j: make(j, z, ring(z + j, NZ)), lambda j: make(j, ring(z - j, NZ), ring(z + j, NZ)))

    def gather(ref, send, recv):
        def far_copy(d):
            return copy(
                ref.at[0, rows(z)], ref.at[d, rows(z)], send.at[d], recv.at[d], at_y(ring(y - d, NY))
            )

        def near_copy(i):
            d = near_d(i)
            return copy(ref.at[0], ref.at[d], send.at[d], recv.at[d], at_y(ring(y - d, NY)))

        def pass_copy(j, source, target):
            part = ref.at[pl.ds(3, 3), rows(source)]
            return copy(part, part, send.at[8 + j], recv.at[8 + j], at_z(target))

        return Copies(3, 6, far_copy, far_copy), Copies(0, 4, near_copy, near_copy), over_z(pass_copy)

    s_far, s_near, s_pass = gather(s_all, ss, sr)

    def step(k):
        def hand_on(i):
            side, half = i % 2, pl.ds(i // 2 * (B // 2), B // 2)
            there, here = (k, k - 1) if side == 0 else (NY - k, (NY + 1 - k) % NY)
            to = at_y(ring(y - 1, NY)) if side == 0 else at_y(ring(y + 1, NY))
            index = 4 * (k - 1) + i
            return copy(t_all.at[here, half], t_all.at[there, half], ts.at[index], tr.at[index], to)

        return Copies(0, 4, hand_on, hand_on)

    def t_piece_copy(i):
        part = (4, rows(z))
        return copy(t_all.at[0, rows(z)], t_all.at[part], ts.at[12], tr.at[12], at_y(ring(y + 4, NY)))

    def t_pass_copy(j, source, target):
        part = t_all.at[4, rows(source)]
        return copy(part, part, ts.at[12 + j], tr.at[12 + j], at_z(target))

    t_steps = [step(k) for k in (1, 2, 3)]
    t_piece, t_pass = Copies(0, 1, t_piece_copy, t_piece_copy), over_z(t_pass_copy)

    def x_copy(j, source, target):
        part = p_all.at[core * NX + source]
        return copy(part, part, ps.at[j], pr.at[j], at_p(core * NX + target))

    def over_x(make):
        return Copies(1, NX, lambda j: make(j, x, ring(x + j, NX)), lambda j: make(j, ring(x - j, NX), ring(x + j, NX)))

    def sib_copy(j, who):
        part = p_all.at[who * NX + ring(x - j, NX)]
        return copy(part, part, ps.at[4 + j], pr.at[4 + j], at_p((1 - core) * NX + x))

    p_x = over_x(x_copy)
    p_own = Copies(0, 1, lambda j: sib_copy(j, core), lambda j: sib_copy(j, 1 - core))
    p_passed = Copies(1, NX, lambda j: sib_copy(j, core), lambda j: sib_copy(j, 1 - core))

    t_piece.start()
    p_x.start()
    t_steps[0].start_all()
    p_own.start()
    for now, later in zip(t_steps, t_steps[1:]):
        log.append(later)
        for i in range(4):
            now.recv_one(i)
            later.out(i).start()
        if later is t_steps[1]:
            s_far.start()
            t_piece.recv()
            t_pass.start()
    p_x.recv()
    p_passed.start()
    p_own.recv()
    s_far.recv()
    s_pass.start()
    s_near.start()
    p_passed.recv()

    def proto_pair(n):
        return p_all[2 * n : 2 * n + 2].reshape(2 * B, K)

    col_now[...] = jnp.zeros((8, C), F32)

    def teacher_block(d):
        block = t_all[d]
        for n in range(C // 256):
            lanes = slice(n * 256, (n + 1) * 256)
            expo = jnp.exp(against_rows(block, proto_pair(n)) * TEACHER)
            e_ref[crop_rows(d), lanes] = expo
            col_now[:, lanes] += jnp.sum(expo.reshape(B // 8, 8, 256), axis=0)

    for d in (0, 1, 7, 2, 6):
        teacher_block(d)
    for i in range(4):
        t_steps[2].recv_one(i)
    for d in (3, 5):
        teacher_block(d)
    t_pass.recv()
    teacher_block(4)

    class Swap(Copies):
        def __init__(self, buf, send, recv, mine, at):
            def out(q):
                return copy(buf.at[mine], buf.at[mine], send.at[q], recv.at[mine], at(ring(mine + q, 8)))

            def into(q):
                source = ring(mine + q, 8)
                return copy(buf.at[source], buf.at[source], send.at[q], recv.at[source], at(source))

            super().__init__(1, 8, out, into)
            self.buf = buf

        def start(self):
            log.append(self)
            for q in (4, 3, 5, 2, 6, 1, 7):
                self.out(q).start()

        def total(self):
            self.left.clear()
            for q in (1, 7, 2, 6, 3, 5, 4):
                self.into(q).wait_recv()
            total = self.buf[0]
            for i in range(1, 8):
                total = total + self.buf[i]
            return total

    col_swap = [Swap(colx.at[it], xs.at[it], xr.at[it], own, at_p) for it in range(3)]
    y_swap = [Swap(rowy.at[it], ys.at[it], yr.at[it], y, at_y) for it in range(2)]
    z_swap = [Swap(rowz.at[it], zs.at[it], zr.at[it], z, at_z) for it in range(2)]
    last_y = Swap(rowy.at[2], ys.at[2], yr.at[2], y, at_y)
    last_z = Swap(rowz.at[2], zs.at[2], zr.at[2], z, at_z)
    student_y = Swap(rowy.at[3], ys.at[3], yr.at[3], y, at_y)
    student_z = Swap(rowz.at[3], zs.at[3], zr.at[3], z, at_z)
    mixed_y = Swap(rowy.at[4], ys.at[4], yr.at[4], y, at_y)
    mixed_z = Swap(rowz.at[4], zs.at[4], zr.at[4], z, at_z)

    def lane_rows(tile):
        return jnp.sum(tile.T, axis=0, keepdims=True)

    def down(vector):
        return jnp.broadcast_to(vector, (B, B)).T

    def lane_tile(k):
        return slice(k * B, (k + 1) * B)

    def times_protos(d):
        return jnp.dot(g_ref[crop_rows(d), :], p_all[...].reshape(C, K), preferred_element_type=F32)

    class Reduce:
        def __init__(self, u, u_own, near, zfar, w, yfar, b, b16, zn, send, recv):
            self.bufs = u, u_own, near, zfar, w, yfar, b, zn
            self.b16 = b16

            def far_copy(j, source, target):
                part = u.at[pl.ds(3, 3), rows(target)]
                return copy(part, zfar.at[source], send.at[j], recv.at[j], at_z(target))

            def near_copy(i):
                d = near_d(i)
                return copy(u.at[d], near.at[i], send.at[8 + i], recv.at[8 + i], at_y(ring(y + d, NY)))

            def sum_copy(k):
                to = at_y(ring(y + 3 + k, NY))
                return copy(w.at[k], yfar.at[k], send.at[12 + k], recv.at[12 + k], to)

            def piece_copy(j, source, target):
                return copy(b16.at[rows(target)], zn.at[source], send.at[16 + j], recv.at[16 + j], at_z(target))

            self.far, self.piece = over_z(far_copy), over_z(piece_copy)
            self.near, self.sum = Copies(0, 4, near_copy, near_copy), Copies(0, 3, sum_copy, sum_copy)

        def put(self, d, block):
            u, u_own = self.bufs[:2]
            if isinstance(d, int) and d == 0:
                u_own[...] = block
            else:
                u[d] = block.astype(BF16)

        def far_sums(self):
            u, _, _, zfar, w, _, _, _ = self.bufs
            self.far.recv()
            zfar[z] = u[pl.ds(3, 3), rows(z)]
            total = zfar[0].astype(F32)
            for i in range(1, NZ):
                total = total + zfar[i].astype(F32)
            w[...] = total.astype(BF16)
            self.sum.start()

        def near_sums(self):
            _, u_own, near, _, _, _, b, _ = self.bufs
            self.near.recv()
            b[...] = u_own[...] + sum(near[i].astype(F32) for i in range(4))
            self.b16[...] = b[...].astype(BF16)
            self.piece.start()

        def result(self):
            _, _, _, _, _, yfar, b, zn = self.bufs
            self.piece.recv()
            self.sum.recv()
            zn[z] = jnp.zeros((PIECE, K), BF16)
            total = b[rows(z)] + sum(yfar[i].astype(F32) for i in range(3))
            for i in range(NZ):
                total = total + zn[i].astype(F32)
            return total

    s_reduce = Reduce(us_ref, us_own, s_near_in, s_zfar, s_w, s_yfar, s_b, s_b16, s_zn, uss, usr)
    t_reduce = Reduce(ut_ref, ut_own, t_near_in, t_zfar, t_w, t_yfar, t_b, t_b16, t_zn, uts, utr)

    def student_block(d):
        block = s_all[d]
        total = jnp.zeros((B, B), F32)
        for n in range(C // 256):
            lanes = slice(n * 256, (n + 1) * 256)
            logits = against_rows(block, proto_pair(n)) * STUDENT
            expo = jnp.exp(logits)
            l_ref[crop_rows(d), lanes] = logits
            x_ref[crop_rows(d), lanes] = expo
            g_ref[crop_rows(d), lanes] = expo.astype(BF16)
            total = total + expo[:, :B] + expo[:, B:]
        rowy[3, y, pl.ds(ring(y + d, NY), 1), :] = lane_rows(total)
        s_turned[:, crop_rows(d)] = block.T
        s_reduce.put(d, times_protos(d))

    def near_student(i):
        s_near.recv_one(i)
        student_block(near_d(i))

    def weigh_rows(it):
        scale = col_now[:, :B]

        def block(d):
            total = jnp.zeros((B, B), F32)
            for k in range(NP):
                total = total + e_ref[crop_rows(d), lane_tile(k)] * scale[k : k + 1, :]
            rowy[it, y, pl.ds(ring(y + d, NY), 1), :] = lane_rows(total)

        each(0, NY, block, 8)

    def weigh_columns(it):
        def block(d, totals):
            scale = down(row_now[pl.ds(ring(y + d, NY), 1), :])
            return tuple(
                totals[k]
                + jnp.sum((e_ref[crop_rows(d), lane_tile(k)] * scale).reshape(B // 8, 8, B), axis=0)
                for k in range(NP)
            )

        totals = lax.fori_loop(0, NY, block, (jnp.zeros((8, B), F32),) * NP, unroll=8)
        for k in range(NP):
            colx[it, own, k : k + 1, :] = jnp.sum(totals[k], axis=0, keepdims=True)

    for k in range(NP):
        colx[0, own, k : k + 1, :] = jnp.sum(col_now[:, lane_tile(k)], axis=0, keepdims=True)
    col_swap[0].start()
    student_block(0)
    col_now[:, :B] = 1.0 / col_swap[0].total()
    for it in range(2):
        weigh_rows(it)
        y_swap[it].start()
        if it == 0:
            near_student(0)
            near_student(1)
            near_student(2)
            near_student(3)
        rowz[it, z] = y_swap[it].total()
        z_swap[it].start()
        if it == 0:
            s_reduce.near.start()
        if it == 0:
            s_pass.recv()
            each(3, 6, student_block, 3)
        row_now[...] = 1.0 / z_swap[it].total()
        if it == 0:
            student_y.start()
            s_reduce.far.start()
        else:
            rowz[3, z] = student_y.total()
            student_z.start()
            s_reduce.far_sums()
            s_reduce.near_sums()
        weigh_columns(it + 1)
        col_swap[it + 1].start()
        col_now[:, :B] = 1.0 / col_swap[it + 1].total()

    def last_rows(d):
        scale = col_now[:, :B]
        total = jnp.zeros((B, B), F32)
        for k in range(NP):
            total = total + e_ref[crop_rows(d), lane_tile(k)] * scale[k : k + 1, :]
        rowy[2, y, pl.ds(ring(y + d, NY), 1), :] = lane_rows(total)

    def mixed_rows(d):
        scale = col_now[:, :B]
        mixed = jnp.zeros((B, B), F32)
        for k in range(NP):
            scaled = e_ref[crop_rows(d), lane_tile(k)] * scale[k : k + 1, :]
            mixed = mixed + scaled * l_ref[crop_rows(d), lane_tile(k)]
        rowy[4, y, pl.ds(ring(y + d, NY), 1), :] = lane_rows(mixed)

    def teacher_grad(d):
        scale = col_now[:, :B]
        for k in range(NP):
            g_ref[crop_rows(d), lane_tile(k)] = (
                e_ref[crop_rows(d), lane_tile(k)] * scale[k : k + 1, :]
            ).astype(BF16)
        t_reduce.put(d, times_protos(d))

    each(3, 6, teacher_grad, 3)
    each(0, NY, last_rows, 8)
    last_y.start()
    t_reduce.far.start()

    def near_grad(i):
        teacher_grad(near_d(i))
        t_reduce.near.out(i).start()

    log.append(t_reduce.near)
    each(0, 4, near_grad, 4)
    rowz[2, z] = last_y.total()
    last_z.start()
    teacher_grad(0)
    each(0, NY, mixed_rows, 8)
    mixed_y.start()
    last_now[8:16] = student_z.total()
    last_now[0:8] = last_z.total()
    t_reduce.near_sums()
    t_reduce.far_sums()
    last_now[16:24] = 1.0 / last_now[0:8]
    last_now[24:32] = 1.0 / last_now[8:16]
    down_ref[0] = down(last_now[pl.ds(16 + y, 1), :])
    down_ref[1] = down(last_now[pl.ds(24 + y, 1), :])

    def grad_block(d):
        b = ring(y + d, NY)
        scale = col_now[:, :B]
        row_scale, student_scale = down(last_now[pl.ds(16 + b, 1), :]), down(last_now[pl.ds(24 + b, 1), :])
        for k in range(NP):
            target = e_ref[crop_rows(d), lane_tile(k)] * scale[k : k + 1, :] * row_scale
            g_ref[crop_rows(d), lane_tile(k)] = (
                x_ref[crop_rows(d), lane_tile(k)] * student_scale - target
            ).astype(BF16)

    each(0, NY, grad_block, 8)

    def proto_grad(half):
        def pair(n):
            first = pl.multiple_of((half * 2 + n) * 256, 256)
            both = jnp.dot(s_turned[...], g_ref[:, pl.ds(first, 256)], preferred_element_type=F32)
            v_ref[half * NX + 2 * n] = both[:, :B]
            v_ref[half * NX + 2 * n + 1] = both[:, B:]

        each(0, 2, pair)

    def v_sib_copy(who):
        return copy(v_ref.at[pl.ds(who * NX, NX)], vsib, vs.at[0], vr.at[0], at_p((1 - core) * NX + x))

    def v_x_copy(j, source, target):
        return copy(v_out.at[target], vx.at[source], vs.at[j], vr.at[j], at_p(core * NX + target))

    v_sib = Copies(0, 1, lambda i: v_sib_copy(1 - core), lambda i: v_sib_copy(1 - core))
    v_x = over_x(v_x_copy)

    proto_grad(1 - core)
    v_sib.start()
    rowz[4, z] = mixed_y.total()
    mixed_z.start()
    proto_grad(core)

    v_sib.recv()

    def add_sibling(i):
        total = v_ref[core * NX + i] + vsib[i]
        v_ref[core * NX + i] = total
        v_out[i] = total.astype(BF16)

    each(0, NX, add_sibling, 4)
    v_x.start()
    student_part = s_reduce.result() * down_ref[1, rows(z), 0:1]
    teacher_part = t_reduce.result() * down_ref[0, rows(z), 0:1]
    unit_grad = (student_part - teacher_part) * (STUDENT / CROPS)
    gfb[rows(z)] = project(su_ref[rows(z)], unit_grad, sinv_ref[rows(z), 0:1])

    def all_copy(j, source, target):
        part = gfb.at[rows(source)]
        return copy(part, part, gs.at[j], gr.at[j], at_z(target))

    every = over_z(all_copy)
    every.start()
    row_now[...] = jnp.log(last_now[8:16]) - mixed_z.total() * last_now[16:24]
    loss_ref[...] = row_now[pl.ds(y, 1), :]

    v_x.recv()
    vx[x] = jnp.zeros((K, B), BF16)
    proto_sum = (v_ref[own] + sum(vx[i].astype(F32) for i in range(NX))).T * (STUDENT / CROPS)
    gp_ref[...] = project(pu_ref[...], proto_sum, pinv_ref[:, 0:1])
    every.recv()
    gf_ref[...] = gfb[...]

    for group in log:
        group.sent()


def reduce_shapes():
    return [
        pltpu.VMEM((NY, B, K), BF16),
        pltpu.VMEM((B, K), F32),
        pltpu.VMEM((4, B, K), BF16),
        pltpu.VMEM((NZ, 3, PIECE, K), BF16),
        pltpu.VMEM((3, PIECE, K), BF16),
        pltpu.VMEM((3, PIECE, K), BF16),
        pltpu.VMEM((B, K), F32),
        pltpu.VMEM((B, K), BF16),
        pltpu.VMEM((NZ, PIECE, K), BF16),
    ]


def shards(student_features, teacher_features, prototypes):
    vmem = pl.BlockSpec(memory_space=pltpu.VMEM)
    dma = pltpu.SemaphoreType.DMA
    grad_features, grad_prototypes, losses = pl.pallas_call(
        kernel,
        out_shape=(
            jax.ShapeDtypeStruct((B, K), F32),
            jax.ShapeDtypeStruct((B, K), F32),
            jax.ShapeDtypeStruct((1, B), F32),
        ),
        in_specs=[pl.BlockSpec(memory_space=pltpu.MemorySpace.HBM)] * 3,
        out_specs=(vmem,) * 3,
        scratch_shapes=[
            pltpu.VMEM((B, K), BF16), pltpu.VMEM((B, K), BF16), pltpu.VMEM((B, K), BF16),
            pltpu.VMEM((NY, B, K), BF16),
            pltpu.VMEM((NY, B, K), BF16),
            pltpu.VMEM((K, R), BF16),
            pltpu.VMEM((NP, B, K), BF16),
            pltpu.VMEM((R, C), F32),
            pltpu.VMEM((R, C), F32),
            pltpu.VMEM((R, C), F32),
            pltpu.VMEM((R, C), BF16),
            pltpu.VMEM((B, K), F32),
            pltpu.VMEM((B, K), F32),
            pltpu.VMEM((B, 128), F32),
            pltpu.VMEM((B, 128), F32),
            pltpu.VMEM((3, 8, 8, 128), F32),
            pltpu.VMEM((5, 8, 8, 128), F32),
            pltpu.VMEM((5, 8, 8, 128), F32),
            pltpu.VMEM((8, C), F32),
            pltpu.VMEM((8, 128), F32),
            pltpu.VMEM((32, 128), F32),
            pltpu.VMEM((2, B, 128), F32),
            *reduce_shapes(),
            *reduce_shapes(),
            pltpu.VMEM((B, K), F32),
            pltpu.VMEM((NP, K, B), F32),
            pltpu.VMEM((NX, K, B), F32),
            pltpu.VMEM((NX, K, B), BF16),
            pltpu.VMEM((NX, K, B), BF16),
            dma((3,)),
            dma((20,)), dma((20,)),
            dma((16,)), dma((16,)),
            dma((8,)), dma((8,)),
            dma((3, 8)), dma((3, 8)),
            dma((5, 8)), dma((5, 8)),
            dma((5, 8)), dma((5, 8)),
            dma((24,)), dma((24,)),
            dma((24,)), dma((24,)),
            dma((8,)), dma((8,)),
            dma((4,)), dma((4,)),
        ],
        compiler_params=pltpu.CompilerParams(
            collective_id=0, has_side_effects=True, vmem_limit_bytes=50 * 1024 * 1024
        ),
        name="dino_head",
    )(*(pltpu.with_memory_space_constraint(a, pltpu.MemorySpace.HBM) for a in (student_features, teacher_features, prototypes)))
    return grad_features, grad_prototypes, losses.reshape(B)


def solution(mesh):
    in_specs = (P("dp", None), P("dp", None), P(("dp", "proto"), None))
    out_specs = (P("dp", None), P(("dp", "proto"), None), P("dp"))
    return jax.shard_map(shards, mesh=mesh, in_specs=in_specs, out_specs=out_specs, check_vma=False)
```

```python
import jax
import jax.numpy as jnp
from jax import lax
from jax.experimental import pallas as pl
from jax.experimental.pallas import tpu as pltpu
from jax.sharding import PartitionSpec as P

NY, NX, NC, NZ = 8, 4, 2, 8
NP = NX * NC
B = 128
K = 384
R = NY * B
C = NP * B
PIECE = B // NZ
CROPS = NY * NX * NC * B
TEACHER = 1.0 / 0.07
STUDENT = 1.0 / 0.1
EPS = 1e-06
MESH = pl.DeviceIdType.MESH
F32, BF16 = jnp.float32, jnp.bfloat16


def unit_rows(values):
    widened = values.astype(F32)
    inverse = lax.rsqrt(jnp.sum(widened * widened, axis=-1, keepdims=True) + EPS)
    return widened * inverse, inverse


def against_rows(a, b):
    return lax.dot_general(a, b, (((1,), (1,)), ((), ())), preferred_element_type=F32)


def project(unit, grad, inverse):
    return inverse * (grad - unit * jnp.sum(unit * grad, axis=1, keepdims=True))


def kernel(
    s_hbm, t_hbm, p_hbm, gf_ref, gp_ref, loss_ref,
    s_ref, t_ref, p_ref,
    t_all, s_all, s_turned, p_all, e_ref, l_ref, x_ref, g_ref, su_ref, pu_ref, sinv_ref, pinv_ref,
    colx, rowy, rowz, col_now, row_now, last_now,
    down_ref, us_ref, us_own, s_near_in, s_zfar, s_w, s_yfar, s_b, s_b16, s_zn,
    ut_ref, ut_own, t_near_in, t_zfar, t_w, t_yfar, t_b, t_b16, t_zn, gfb, v_ref, vsib, v_out, v_opposite_in, vx,
    ins, ts, tr, ss, sr, ps, pr, xs, xr, ys, yr, zs, zr, uss, usr, uts, utr, gs, gr, vs, vr,
):
    dp, z = lax.axis_index("dp"), lax.axis_index("proto")
    core = lax.rem(dp, NC)
    x = lax.rem(lax.div(dp, NC), NX)
    y = lax.div(dp, NC * NX)
    own = core * NX + x

    def at_y(other):
        return ((other * NX + x) * NC + core, z)

    def at_z(other):
        return (dp, other)

    def at_p(other):
        return ((y * NX + lax.rem(other, NX)) * NC + lax.div(other, NX), z)

    def ring(value, size):
        return lax.rem(value + size, size)

    def copy(src, dst, send, recv, device):
        return pltpu.make_async_remote_copy(
            src_ref=src, dst_ref=dst, send_sem=send, recv_sem=recv, device_id=device, device_id_type=MESH
        )

    def each(first, last, body, unroll=1):
        def step(i, carry):
            body(i)
            return carry

        lax.fori_loop(first, last, step, 0, unroll=unroll)

    loads = [
        pltpu.make_async_copy(far, here, ins.at[i])
        for i, (far, here) in enumerate(((t_hbm, t_ref), (p_hbm, p_ref), (s_hbm, s_ref)))
    ]
    for load in loads:
        load.start()

    barrier = pltpu.get_barrier_semaphore()

    def greet(q):
        for device in (at_y(ring(y + q, NY)), at_p(ring(own + q, NP)), at_z(ring(z + q, NZ))):
            pl.semaphore_signal(barrier, inc=1, device_id=device, device_id_type=MESH)

    each(1, 8, greet)

    for load in loads:
        load.wait()
    t_all[0] = unit_rows(t_ref[...])[0].astype(BF16)
    p_unit, p_inverse = unit_rows(p_ref[...])
    p_all[own] = p_unit.astype(BF16)
    pu_ref[...] = p_unit
    pinv_ref[...] = jnp.broadcast_to(p_inverse, (B, 128))
    s_unit, s_inverse = unit_rows(s_ref[...])
    s_all[0] = s_unit.astype(BF16)
    su_ref[...] = s_unit
    sinv_ref[...] = jnp.broadcast_to(s_inverse, (B, 128))
    pl.semaphore_wait(barrier, 21)

    log = []

    class Copies:
        def __init__(self, first, last, out, into):
            self.first, self.last, self.out, self.into = first, last, out, into
            self.left = set(range(first, last))

        def start(self):
            log.append(self)
            each(self.first, self.last, lambda i: self.out(i).start())

        def start_all(self):
            log.append(self)
            for i in range(self.first, self.last):
                self.out(i).start()

        def recv(self):
            self.left.clear()
            each(self.first, self.last, lambda i: self.into(i).wait_recv())

        def recv_one(self, i):
            if isinstance(i, int):
                self.left.discard(i)
            else:
                self.left.clear()
            self.into(i).wait_recv()

        def sent(self):
            for i in range(self.first, self.last):
                self.out(i).wait_send()

    def rows(who):
        return pl.ds(pl.multiple_of(who * PIECE, PIECE), PIECE)

    def crop_rows(d):
        return pl.ds(pl.multiple_of(d * B, B), B)

    def near_d(i):
        return ring((lax.div(i, 2) + 1) * (1 - 2 * lax.rem(i, 2)), NY)

    def over_z(make):
        return Copies(1, NZ, lambda j: make(j, z, ring(z + j, NZ)), lambda j: make(j, ring(z - j, NZ), ring(z + j, NZ)))

    def gather(ref, send, recv):
        def far_copy(d):
            return copy(
                ref.at[0, rows(z)], ref.at[d, rows(z)], send.at[d], recv.at[d], at_y(ring(y - d, NY))
            )

        def near_copy(i):
            d = near_d(i)
            return copy(ref.at[0], ref.at[d], send.at[d], recv.at[d], at_y(ring(y - d, NY)))

        def pass_copy(j, source, target):
            part = ref.at[pl.ds(3, 3), rows(source)]
            return copy(part, part, send.at[8 + j], recv.at[8 + j], at_z(target))

        return Copies(3, 6, far_copy, far_copy), Copies(0, 4, near_copy, near_copy), over_z(pass_copy)

    s_far, s_near, s_pass = gather(s_all, ss, sr)

    def step(k):
        def hand_on(i):
            side, half = i % 2, pl.ds(i // 2 * (B // 2), B // 2)
            there, here = (k, k - 1) if side == 0 else (NY - k, (NY + 1 - k) % NY)
            to = at_y(ring(y - 1, NY)) if side == 0 else at_y(ring(y + 1, NY))
            index = 4 * (k - 1) + i
            return copy(t_all.at[here, half], t_all.at[there, half], ts.at[index], tr.at[index], to)

        return Copies(0, 4, hand_on, hand_on)

    def t_piece_copy(i):
        part = (4, rows(z))
        return copy(t_all.at[0, rows(z)], t_all.at[part], ts.at[12], tr.at[12], at_y(ring(y + 4, NY)))

    def t_pass_copy(j, source, target):
        part = t_all.at[4, rows(source)]
        return copy(part, part, ts.at[12 + j], tr.at[12 + j], at_z(target))

    t_steps = [step(k) for k in (1, 2, 3)]
    t_piece, t_pass = Copies(0, 1, t_piece_copy, t_piece_copy), over_z(t_pass_copy)

    def x_copy(j, source, target):
        part = p_all.at[core * NX + source]
        return copy(part, part, ps.at[j], pr.at[j], at_p(core * NX + target))

    def over_x(make):
        return Copies(1, NX, lambda j: make(j, x, ring(x + j, NX)), lambda j: make(j, ring(x - j, NX), ring(x + j, NX)))

    def sib_copy(j, who):
        part = p_all.at[who * NX + ring(x - j, NX)]
        return copy(part, part, ps.at[4 + j], pr.at[4 + j], at_p((1 - core) * NX + x))

    p_x = over_x(x_copy)
    p_own = Copies(0, 1, lambda j: sib_copy(j, core), lambda j: sib_copy(j, 1 - core))
    p_passed = Copies(1, NX, lambda j: sib_copy(j, core), lambda j: sib_copy(j, 1 - core))

    t_piece.start()
    p_x.start()
    t_steps[0].start_all()
    p_own.start()
    for now, later in zip(t_steps, t_steps[1:]):
        log.append(later)
        for i in range(4):
            now.recv_one(i)
            later.out(i).start()
        if later is t_steps[1]:
            s_far.start()
            t_piece.recv()
            t_pass.start()
    p_x.recv()
    p_passed.start()
    p_own.recv()
    s_far.recv()
    s_pass.start()
    s_near.start()
    p_passed.recv()

    def proto_pair(n):
        return p_all[2 * n : 2 * n + 2].reshape(2 * B, K)

    col_now[...] = jnp.zeros((8, C), F32)

    def teacher_block(d):
        block = t_all[d]
        for n in range(C // 256):
            lanes = slice(n * 256, (n + 1) * 256)
            expo = jnp.exp(against_rows(block, proto_pair(n)) * TEACHER)
            e_ref[crop_rows(d), lanes] = expo
            col_now[:, lanes] += jnp.sum(expo.reshape(B // 8, 8, 256), axis=0)

    for d in (0, 1, 7, 2, 6):
        teacher_block(d)
    for i in range(4):
        t_steps[2].recv_one(i)
    for d in (3, 5):
        teacher_block(d)
    t_pass.recv()
    teacher_block(4)

    class Swap(Copies):
        def __init__(self, buf, send, recv, mine, at):
            def out(q):
                return copy(buf.at[mine], buf.at[mine], send.at[q], recv.at[mine], at(ring(mine + q, 8)))

            def into(q):
                source = ring(mine + q, 8)
                return copy(buf.at[source], buf.at[source], send.at[q], recv.at[source], at(source))

            super().__init__(1, 8, out, into)
            self.buf = buf

        def start(self):
            log.append(self)
            for q in (4, 3, 5, 2, 6, 1, 7):
                self.out(q).start()

        def total(self):
            self.left.clear()
            for q in (1, 7, 2, 6, 3, 5, 4):
                self.into(q).wait_recv()
            total = self.buf[0]
            for i in range(1, 8):
                total = total + self.buf[i]
            return total

    col_swap = [Swap(colx.at[it], xs.at[it], xr.at[it], own, at_p) for it in range(3)]
    y_swap = [Swap(rowy.at[it], ys.at[it], yr.at[it], y, at_y) for it in range(2)]
    z_swap = [Swap(rowz.at[it], zs.at[it], zr.at[it], z, at_z) for it in range(2)]
    last_y = Swap(rowy.at[2], ys.at[2], yr.at[2], y, at_y)
    last_z = Swap(rowz.at[2], zs.at[2], zr.at[2], z, at_z)
    student_y = Swap(rowy.at[3], ys.at[3], yr.at[3], y, at_y)
    student_z = Swap(rowz.at[3], zs.at[3], zr.at[3], z, at_z)
    mixed_y = Swap(rowy.at[4], ys.at[4], yr.at[4], y, at_y)
    mixed_z = Swap(rowz.at[4], zs.at[4], zr.at[4], z, at_z)

    def lane_rows(tile):
        return jnp.sum(tile.T, axis=0, keepdims=True)

    def down(vector):
        return jnp.broadcast_to(vector, (B, B)).T

    def lane_tile(k):
        return slice(k * B, (k + 1) * B)

    def times_protos(d):
        return jnp.dot(g_ref[crop_rows(d), :], p_all[...].reshape(C, K), preferred_element_type=F32)

    class Reduce:
        def __init__(self, u, u_own, near, zfar, w, yfar, b, b16, zn, send, recv):
            self.bufs = u, u_own, near, zfar, w, yfar, b, zn
            self.b16 = b16

            def far_copy(j, source, target):
                part = u.at[pl.ds(3, 3), rows(target)]
                return copy(part, zfar.at[source], send.at[j], recv.at[j], at_z(target))

            def near_copy(i):
                d = near_d(i)
                return copy(u.at[d], near.at[i], send.at[8 + i], recv.at[8 + i], at_y(ring(y + d, NY)))

            def sum_copy(k):
                to = at_y(ring(y + 3 + k, NY))
                return copy(w.at[k], yfar.at[k], send.at[12 + k], recv.at[12 + k], to)

            def piece_copy(j, source, target):
                return copy(b16.at[rows(target)], zn.at[source], send.at[16 + j], recv.at[16 + j], at_z(target))

            self.far, self.piece = over_z(far_copy), over_z(piece_copy)
            self.near, self.sum = Copies(0, 4, near_copy, near_copy), Copies(0, 3, sum_copy, sum_copy)

        def put(self, d, block):
            u, u_own = self.bufs[:2]
            if isinstance(d, int) and d == 0:
                u_own[...] = block
            else:
                u[d] = block.astype(BF16)

        def far_sums(self):
            u, _, _, zfar, w, _, _, _ = self.bufs
            self.far.recv()
            zfar[z] = u[pl.ds(3, 3), rows(z)]
            total = zfar[0].astype(F32)
            for i in range(1, NZ):
                total = total + zfar[i].astype(F32)
            w[...] = total.astype(BF16)
            self.sum.start()

        def near_sums(self):
            _, u_own, near, _, _, _, b, _ = self.bufs
            self.near.recv()
            b[...] = u_own[...] + sum(near[i].astype(F32) for i in range(4))
            self.b16[...] = b[...].astype(BF16)
            self.piece.start()

        def result(self):
            _, _, _, _, _, yfar, b, zn = self.bufs
            self.piece.recv()
            self.sum.recv()
            zn[z] = jnp.zeros((PIECE, K), BF16)
            total = b[rows(z)] + sum(yfar[i].astype(F32) for i in range(3))
            for i in range(NZ):
                total = total + zn[i].astype(F32)
            return total

    s_reduce = Reduce(us_ref, us_own, s_near_in, s_zfar, s_w, s_yfar, s_b, s_b16, s_zn, uss, usr)
    t_reduce = Reduce(ut_ref, ut_own, t_near_in, t_zfar, t_w, t_yfar, t_b, t_b16, t_zn, uts, utr)

    def student_block(d):
        block = s_all[d]
        total = jnp.zeros((B, B), F32)
        for n in range(C // 256):
            lanes = slice(n * 256, (n + 1) * 256)
            logits = against_rows(block, proto_pair(n)) * STUDENT
            expo = jnp.exp(logits)
            l_ref[crop_rows(d), lanes] = logits
            x_ref[crop_rows(d), lanes] = expo
            g_ref[crop_rows(d), lanes] = expo.astype(BF16)
            total = total + expo[:, :B] + expo[:, B:]
        rowy[3, y, pl.ds(ring(y + d, NY), 1), :] = lane_rows(total)
        s_turned[:, crop_rows(d)] = block.T
        s_reduce.put(d, times_protos(d))

    def near_student(i):
        s_near.recv_one(i)
        student_block(near_d(i))

    def weigh_rows(it):
        scale = col_now[:, :B]

        def block(d):
            total = jnp.zeros((B, B), F32)
            for k in range(NP):
                total = total + e_ref[crop_rows(d), lane_tile(k)] * scale[k : k + 1, :]
            rowy[it, y, pl.ds(ring(y + d, NY), 1), :] = lane_rows(total)

        each(0, NY, block, 8)

    def weigh_columns(it):
        def block(d, totals):
            scale = down(row_now[pl.ds(ring(y + d, NY), 1), :])
            return tuple(
                totals[k]
                + jnp.sum((e_ref[crop_rows(d), lane_tile(k)] * scale).reshape(B // 8, 8, B), axis=0)
                for k in range(NP)
            )

        totals = lax.fori_loop(0, NY, block, (jnp.zeros((8, B), F32),) * NP, unroll=8)
        for k in range(NP):
            colx[it, own, k : k + 1, :] = jnp.sum(totals[k], axis=0, keepdims=True)

    for k in range(NP):
        colx[0, own, k : k + 1, :] = jnp.sum(col_now[:, lane_tile(k)], axis=0, keepdims=True)
    col_swap[0].start()
    student_block(0)
    col_now[:, :B] = 1.0 / col_swap[0].total()
    for it in range(2):
        weigh_rows(it)
        y_swap[it].start()
        if it == 0:
            near_student(0)
            near_student(1)
            near_student(2)
            near_student(3)
        rowz[it, z] = y_swap[it].total()
        z_swap[it].start()
        if it == 0:
            s_reduce.near.start()
        if it == 0:
            s_pass.recv()
            each(3, 6, student_block, 3)
        row_now[...] = 1.0 / z_swap[it].total()
        if it == 0:
            student_y.start()
            s_reduce.far.start()
        else:
            rowz[3, z] = student_y.total()
            student_z.start()
            s_reduce.far_sums()
            s_reduce.near_sums()
        weigh_columns(it + 1)
        col_swap[it + 1].start()
        col_now[:, :B] = 1.0 / col_swap[it + 1].total()

    def last_rows(d):
        scale = col_now[:, :B]
        total = jnp.zeros((B, B), F32)
        for k in range(NP):
            total = total + e_ref[crop_rows(d), lane_tile(k)] * scale[k : k + 1, :]
        rowy[2, y, pl.ds(ring(y + d, NY), 1), :] = lane_rows(total)

    def mixed_rows(d):
        scale = col_now[:, :B]
        mixed = jnp.zeros((B, B), F32)
        for k in range(NP):
            scaled = e_ref[crop_rows(d), lane_tile(k)] * scale[k : k + 1, :]
            mixed = mixed + scaled * l_ref[crop_rows(d), lane_tile(k)]
        rowy[4, y, pl.ds(ring(y + d, NY), 1), :] = lane_rows(mixed)

    def teacher_grad(d):
        scale = col_now[:, :B]
        for k in range(NP):
            g_ref[crop_rows(d), lane_tile(k)] = (
                e_ref[crop_rows(d), lane_tile(k)] * scale[k : k + 1, :]
            ).astype(BF16)
        t_reduce.put(d, times_protos(d))

    each(3, 6, teacher_grad, 3)
    each(0, NY, last_rows, 8)
    last_y.start()
    t_reduce.far.start()

    def near_grad(i):
        teacher_grad(near_d(i))
        t_reduce.near.out(i).start()

    log.append(t_reduce.near)
    each(0, 4, near_grad, 4)
    rowz[2, z] = last_y.total()
    last_z.start()
    teacher_grad(0)
    each(0, NY, mixed_rows, 8)
    mixed_y.start()
    last_now[8:16] = student_z.total()
    last_now[0:8] = last_z.total()
    t_reduce.near_sums()
    t_reduce.far_sums()
    last_now[16:24] = 1.0 / last_now[0:8]
    last_now[24:32] = 1.0 / last_now[8:16]
    down_ref[0] = down(last_now[pl.ds(16 + y, 1), :])
    down_ref[1] = down(last_now[pl.ds(24 + y, 1), :])

    def grad_block(d):
        b = ring(y + d, NY)
        scale = col_now[:, :B]
        row_scale, student_scale = down(last_now[pl.ds(16 + b, 1), :]), down(last_now[pl.ds(24 + b, 1), :])
        for k in range(NP):
            target = e_ref[crop_rows(d), lane_tile(k)] * scale[k : k + 1, :] * row_scale
            g_ref[crop_rows(d), lane_tile(k)] = (
                x_ref[crop_rows(d), lane_tile(k)] * student_scale - target
            ).astype(BF16)

    each(0, NY, grad_block, 8)

    def proto_grad(half):
        def pair(n):
            first = pl.multiple_of((half * 2 + n) * 256, 256)
            both = jnp.dot(s_turned[...], g_ref[:, pl.ds(first, 256)], preferred_element_type=F32)
            v_ref[half * NX + 2 * n] = both[:, :B]
            v_ref[half * NX + 2 * n + 1] = both[:, B:]

        each(0, 2, pair)

    def v_sib_copy(who):
        return copy(v_ref.at[pl.ds(who * NX, NX)], vsib, vs.at[0], vr.at[0], at_p((1 - core) * NX + x))

    def v_x_copy(j, source, target):
        return copy(
            v_ref.at[core * NX + target], vx.at[source], vs.at[j], vr.at[j], at_p(core * NX + target)
        )

    def v_opposite_copy(i):
        return copy(v_out, v_opposite_in, vs.at[2], vr.at[2], at_p(core * NX + ring(x + 2, NX)))

    v_sib = Copies(0, 1, lambda i: v_sib_copy(1 - core), lambda i: v_sib_copy(1 - core))
    v_x = Copies(
        0,
        2,
        lambda i: v_x_copy(1 + 2 * i, x, ring(x + 1 + 2 * i, NX)),
        lambda i: v_x_copy(1 + 2 * i, ring(x - 1 - 2 * i, NX), ring(x + 1 + 2 * i, NX)),
    )
    v_opposite = Copies(0, 1, v_opposite_copy, v_opposite_copy)

    proto_grad(1 - core)
    v_sib.start()
    rowz[4, z] = mixed_y.total()
    mixed_z.start()
    proto_grad(core)

    v_sib.recv()

    def add_sibling(i):
        v_ref[core * NX + i] += vsib[i]

    each(0, NX, add_sibling, 4)
    v_out[...] = v_ref[core * NX + ring(x + 2, NX)].astype(BF16)
    v_opposite.start()
    v_x.start()
    student_part = s_reduce.result() * down_ref[1, rows(z), 0:1]
    teacher_part = t_reduce.result() * down_ref[0, rows(z), 0:1]
    unit_grad = (student_part - teacher_part) * (STUDENT / CROPS)
    gfb[rows(z)] = project(su_ref[rows(z)], unit_grad, sinv_ref[rows(z), 0:1])

    def all_copy(j, source, target):
        part = gfb.at[rows(source)]
        return copy(part, part, gs.at[j], gr.at[j], at_z(target))

    every = over_z(all_copy)
    every.start()
    row_now[...] = jnp.log(last_now[8:16]) - mixed_z.total() * last_now[16:24]
    loss_ref[...] = row_now[pl.ds(y, 1), :]

    v_x.recv()
    v_opposite.recv()
    proto_sum = v_ref[own] + vx[ring(x + 1, NX)] + vx[ring(x - 1, NX)] + v_opposite_in[...].astype(F32)
    proto_sum = proto_sum.T * (STUDENT / CROPS)
    gp_ref[...] = project(pu_ref[...], proto_sum, pinv_ref[:, 0:1])
    every.recv()
    gf_ref[...] = gfb[...]

    for group in log:
        group.sent()


def reduce_shapes():
    return [
        pltpu.VMEM((NY, B, K), BF16),
        pltpu.VMEM((B, K), F32),
        pltpu.VMEM((4, B, K), BF16),
        pltpu.VMEM((NZ, 3, PIECE, K), BF16),
        pltpu.VMEM((3, PIECE, K), BF16),
        pltpu.VMEM((3, PIECE, K), BF16),
        pltpu.VMEM((B, K), F32),
        pltpu.VMEM((B, K), BF16),
        pltpu.VMEM((NZ, PIECE, K), BF16),
    ]


def shards(student_features, teacher_features, prototypes):
    vmem = pl.BlockSpec(memory_space=pltpu.VMEM)
    dma = pltpu.SemaphoreType.DMA
    grad_features, grad_prototypes, losses = pl.pallas_call(
        kernel,
        out_shape=(
            jax.ShapeDtypeStruct((B, K), F32),
            jax.ShapeDtypeStruct((B, K), F32),
            jax.ShapeDtypeStruct((1, B), F32),
        ),
        in_specs=[pl.BlockSpec(memory_space=pltpu.MemorySpace.HBM)] * 3,
        out_specs=(vmem,) * 3,
        scratch_shapes=[
            pltpu.VMEM((B, K), BF16), pltpu.VMEM((B, K), BF16), pltpu.VMEM((B, K), BF16),
            pltpu.VMEM((NY, B, K), BF16),
            pltpu.VMEM((NY, B, K), BF16),
            pltpu.VMEM((K, R), BF16),
            pltpu.VMEM((NP, B, K), BF16),
            pltpu.VMEM((R, C), F32),
            pltpu.VMEM((R, C), F32),
            pltpu.VMEM((R, C), F32),
            pltpu.VMEM((R, C), BF16),
            pltpu.VMEM((B, K), F32),
            pltpu.VMEM((B, K), F32),
            pltpu.VMEM((B, 128), F32),
            pltpu.VMEM((B, 128), F32),
            pltpu.VMEM((3, 8, 8, 128), F32),
            pltpu.VMEM((5, 8, 8, 128), F32),
            pltpu.VMEM((5, 8, 8, 128), F32),
            pltpu.VMEM((8, C), F32),
            pltpu.VMEM((8, 128), F32),
            pltpu.VMEM((32, 128), F32),
            pltpu.VMEM((2, B, 128), F32),
            *reduce_shapes(),
            *reduce_shapes(),
            pltpu.VMEM((B, K), F32),
            pltpu.VMEM((NP, K, B), F32),
            pltpu.VMEM((NX, K, B), F32),
            pltpu.VMEM((K, B), BF16),
            pltpu.VMEM((K, B), BF16),
            pltpu.VMEM((NX, K, B), F32),
            dma((3,)),
            dma((20,)), dma((20,)),
            dma((16,)), dma((16,)),
            dma((8,)), dma((8,)),
            dma((3, 8)), dma((3, 8)),
            dma((5, 8)), dma((5, 8)),
            dma((5, 8)), dma((5, 8)),
            dma((24,)), dma((24,)),
            dma((24,)), dma((24,)),
            dma((8,)), dma((8,)),
            dma((4,)), dma((4,)),
        ],
        compiler_params=pltpu.CompilerParams(
            collective_id=0, has_side_effects=True, vmem_limit_bytes=50 * 1024 * 1024
        ),
        name="dino_head",
    )(*(pltpu.with_memory_space_constraint(a, pltpu.MemorySpace.HBM) for a in (student_features, teacher_features, prototypes)))
    return grad_features, grad_prototypes, losses.reshape(B)


def solution(mesh):
    in_specs = (P("dp", None), P("dp", None), P(("dp", "proto"), None))
    out_specs = (P("dp", None), P(("dp", "proto"), None), P("dp"))
    return jax.shard_map(shards, mesh=mesh, in_specs=in_specs, out_specs=out_specs, check_vma=False)
```
